256 devices in a mesh: section: 2 (over y_lo), tp: 4 (over x), ep: 32 (over z, y_hi, core).
Axes of the slice: x: 4, y: 4 (y_hi: 2, y_lo: 2; y = y_hi * 2 + y_lo), z: 8, core: 2. Of those that a mesh axis runs over, the one named last changes fastest.
Arguments:
- tokens: bfloat16 [4096, 5120], P(('tp', 'ep'), 'section'), may hold values from -160 to 160
- gain: float32 [5120], P('section'), may hold values from 0.4 to 2.5
- routes: int32 [4096, 6], P(('tp', 'ep')), may hold values from 0 to 127, all different within a row; in each aligned block of 32 rows (0 to 31, 32 to 63, ...) at most 2 rows name the same one
- route_weights: float32 [4096, 6], P(('tp', 'ep')), may hold values from 0.03 to 0.5
- w_gate: bfloat16 [128, 5120, 768], P(('tp', 'ep'), 'section'), may hold values from -0.078125 to 0.078125
- w_up: bfloat16 [128, 5120, 768], P(('tp', 'ep'), 'section'), may hold values from -0.078125 to 0.078125
- w_down: bfloat16 [128, 768, 5120], P(('tp', 'ep'), None, 'section'), may hold values from -0.21875 to 0.21875
- grad_out: bfloat16 [4096, 5120], P(('tp', 'ep'), 'section'), may hold values from -6 to 6
Outputs:
- routed: bfloat16 [4096, 5120], P(('tp', 'ep'), 'section')
- grad_tokens: bfloat16 [4096, 5120], P(('tp', 'ep'), 'section')
- grad_weights: float32 [4096, 6], P(('tp', 'ep'))
The draws below stay inside these ranges and needn't reach their ends.
Inputs may be any that keep to these rules, and one draw needn't show every extreme that they name: `routes`: each row names 6 different experts. In each aligned block of 32 rows (the rows of one index of tp and ep) no expert is named by more than 2 rows, a bound that some block reaches.
All inputs are finite; a program needn't handle non-finite values.
Results may differ from the reference program's by a relative error of at most 0.0072.
Values may be sent and summed in bfloat16 or wider, within the bound.
No kernel may reach another device: no remote copies, remote signals or barrier semaphores. Data moves between devices by JAX's collectives and lax.ppermute only.
A program may use at most 64 MiB of HBM per device.

```python
import math
import jax
import jax.numpy as jnp
import numpy as np
from jax import lax

D = 5120
EXPERT_FF = 768
TOP = 6
TOK_DEV = 32
EXPERTS = 128
CAP_SRC = 2
SLOTS = 256
TOKENS = 4096


def draw_tokens(key, part):
    key = jax.random.fold_in(key, 11)
    key_rows, key_cols, key_vals = jax.random.split(key, 3)
    position = jnp.arange(D, dtype=jnp.float32)[None, :] / D
    row_scale = jnp.exp(jax.random.uniform(key_rows, (TOKENS, 1), jnp.float32, jnp.log(0.3), jnp.log(3.0)))
    col_scale = jnp.exp(jax.random.uniform(key_cols, (1, D), jnp.float32, jnp.log(0.3), jnp.log(3.0)))
    ramp = jnp.exp(position * jnp.log(3.0))
    values = jnp.clip(jax.random.normal(key_vals, (TOKENS, D), jnp.float32), -5.0, 5.0)
    return (values * row_scale * col_scale * ramp).astype(jnp.bfloat16)


def block_levels(stream_key, dims, pieces, low, largest):
    def one(axis_at, shards_of):
        steps = jax.random.uniform(jax.random.fold_in(jax.random.fold_in(stream_key, 6), axis_at), (shards_of,), jnp.float32, low / len(pieces), largest / len(pieces))
        return jnp.repeat(jnp.exp(steps), dims[axis_at] // shards_of).reshape((-1,) + (1,) * (len(dims) - axis_at - 1))

    level = one(*pieces[0])
    for cut in pieces[1:]:
        level = level * one(*cut)
    return level


def assign_block(own_key, own, number, rows, number_of, top, bound, slope):
    order = jax.random.permutation(own_key, number_of)
    crowded, ordinary = shares(number_of, rows * top, bound, slope, True), shares(number_of, rows * top, bound, slope, False)
    places = jnp.arange(number_of)

    def named(lengths, turn):
        used = int((lengths > 0).sum())
        fixed = max(1, used // 4)
        passed = fixed + (places - fixed + turn * (used - fixed)) % max(1, number_of - fixed)
        return jnp.zeros((number_of,), jnp.int32).at[order[jnp.where(places < fixed, places, passed)]].set(jnp.asarray(lengths, jnp.int32))

    lengths = jnp.where(number % 4 == 0, named(crowded, number // 4), named(ordinary, number - number // 4 - 1))
    mixed = jax.random.permutation(jax.random.fold_in(own, 3), number_of)
    giver, sink = mixed[0:number_of // 2 * 2:2], mixed[1:number_of // 2 * 2:2]
    slack = jnp.minimum(lengths[giver] - 1, bound - lengths[sink]) // 2
    slack = jnp.where((giver == order[0]) | (sink == order[0]) | (lengths[sink] == 0), 0, jnp.maximum(slack, 0))
    passed = jax.random.randint(jax.random.fold_in(own, 4), (number_of // 2,), 0, 1 << 20) % (slack + 1)
    lengths = lengths.at[giver].add(-passed).at[sink].add(passed)
    members = jnp.searchsorted(jnp.cumsum(lengths), jnp.arange(rows * top), side="right").astype(jnp.int32)
    grid = members.reshape(top, rows).T
    grid = grid[jax.random.permutation(jax.random.fold_in(own, 1), rows)]
    turn = jax.random.randint(jax.random.fold_in(own, 2), (rows, 1), 0, top)
    return jnp.take_along_axis(grid, (jnp.arange(top)[None, :] + turn) % top, axis=1)


def shares(number_of, total, limit, slope, full):
    portions = [(1 << 20) // math.isqrt(standing ** slope) + 1 for standing in range(1, number_of + 1)]
    largest = limit if full else min(limit, max(-(-total // number_of), total * portions[0] // sum(portions)))
    least = 1 if total - largest >= number_of - 1 else 0
    holding, spare = [largest] + [least] * (number_of - 1), total - largest - least * (number_of - 1)
    while spare > 0:
        movable = [i for i in range(1, number_of) if holding[i] < largest] or [i for i in range(1, number_of) if holding[i] < limit]
        whole, remaining = sum([portions[i] for i in movable]), spare
        for i in movable:
            more = min(limit - holding[i], max(1, remaining * portions[i] // whole), spare)
            holding[i] = holding[i] + more
            spare = spare - more
    return np.array(holding)


def scatter_about(rng, extent, scale, limit, shards=(), kind=jnp.bfloat16):
    level = block_levels(rng, extent, shards, -0.22, 0.18) if shards else 1.0
    result = jax.random.normal(rng, extent, jnp.float32) * scale * level
    return jnp.minimum(jnp.maximum(result, -limit), limit).astype(kind)


def setup_inputs(seed: int = 0) -> dict:
    splits = jax.random.split(jax.random.key(seed), 9)
    tokens = draw_tokens(jax.random.fold_in(splits[8], 71), 0)
    gain = jnp.clip(jnp.exp(math.log(2.5) - 1.8325814 * jax.random.uniform(splits[1], (D,), jnp.float32) ** block_levels(splits[1], (D,), ((0, 2),), -0.2, 0.2)), 0.4, 2.5)
    routes_keys = jax.random.split(jax.random.fold_in(splits[2], 1), TOKENS // TOK_DEV)
    routes_turns = jax.random.permutation(jax.random.fold_in(splits[2], 3), TOKENS // TOK_DEV)
    routes = jax.vmap(lambda own, number: assign_block(jax.random.fold_in(splits[2], 2), own, number, TOK_DEV, EXPERTS, TOP, CAP_SRC, 2))(routes_keys, routes_turns).reshape((TOKENS, TOP))
    route_weights = jnp.clip(jnp.exp(math.log(0.5) - 2.8134107 * jax.random.uniform(splits[3], (TOKENS, TOP), jnp.float32) ** block_levels(splits[3], (TOKENS, TOP), ((0, 128),), -0.2, 0.2)), 0.03, 0.5)
    w_gate = scatter_about(splits[4], (EXPERTS, D, EXPERT_FF), D ** -0.5, 0.078125, ((0, 128), (1, 2)))
    w_up = scatter_about(splits[5], (EXPERTS, D, EXPERT_FF), D ** -0.5, 0.078125, ((0, 128), (1, 2)))
    w_down = scatter_about(splits[6], (EXPERTS, EXPERT_FF, D), EXPERT_FF ** -0.5, 0.21875, ((0, 128), (2, 2)))
    grad_out = scatter_about(splits[7], (TOKENS, D), 1.0, 6.0, ((0, 128), (1, 2)))
    return dict(tokens=tokens, gain=gain, routes=routes, route_weights=route_weights, w_gate=w_gate, w_up=w_up, w_down=w_down, grad_out=grad_out)


EPS = 1e-06

def reference(tokens, gain, routes, route_weights, w_gate, w_up, w_down, grad_out):
    tokens_f = tokens.astype(jnp.float32)
    inv_rms = lax.rsqrt(lax.optimization_barrier(jnp.mean(tokens_f * tokens_f, axis=1, keepdims=True)) + EPS)
    normed = (tokens_f * inv_rms * gain).astype(jnp.bfloat16)
    n_blocks = TOKENS // TOK_DEV
    onehot = (routes[:, :, None] == jnp.arange(EXPERTS, dtype=jnp.int32)[None, None, :]).astype(jnp.int32)
    blockwise = onehot.reshape(n_blocks, TOK_DEV * TOP, EXPERTS)
    before = jnp.cumsum(blockwise, axis=1) - blockwise
    slot_rank = lax.optimization_barrier(jnp.sum(before * blockwise, axis=2)).reshape(TOKENS, TOP)
    block_ids = (jnp.arange(TOKENS, dtype=jnp.int32) // TOK_DEV)[:, None]
    slots = (block_ids * CAP_SRC + slot_rank).astype(jnp.int32)
    assigned = jnp.arange(TOKENS * TOP, dtype=jnp.int32)
    table = jnp.full((EXPERTS, SLOTS), TOKENS * TOP, jnp.int32)
    table = table.at[routes.reshape(-1).astype(jnp.int32), slots.reshape(-1)].set(assigned)
    source_tok = table // TOP
    source_k = table % TOP
    normed_pad = jnp.concatenate([normed, jnp.zeros((1, D), normed.dtype)], axis=0)
    grad_pad = jnp.concatenate([grad_out.astype(jnp.float32), jnp.zeros((1, D), jnp.float32)], axis=0)
    weight_pad = jnp.concatenate([route_weights, jnp.zeros((1, TOP), route_weights.dtype)], axis=0)

    def one_expert(totals, inputs):
        routed_sum, grad_sum, weight_grad = totals
        gate_w, up_w, down_w, rows_tok, rows_k = inputs
        rows = normed_pad[rows_tok]
        pre_gate = jnp.dot(rows, gate_w, preferred_element_type=jnp.float32)
        pre_up = jnp.dot(rows, up_w, preferred_element_type=jnp.float32)
        sigmoid_gate = jax.nn.sigmoid(pre_gate)
        activated = (pre_gate * sigmoid_gate * pre_up).astype(jnp.bfloat16)
        expert_out = jnp.dot(activated, down_w, preferred_element_type=jnp.float32).astype(jnp.bfloat16)
        out_f = expert_out.astype(jnp.float32)
        scale = weight_pad[rows_tok, rows_k][:, None]
        grad_rows = grad_pad[rows_tok]
        routed_sum = routed_sum.at[rows_tok].add(scale * out_f)
        weight_grad = weight_grad.at[rows_tok, rows_k].add(lax.optimization_barrier(jnp.sum(grad_rows * out_f, axis=1)))
        grad_expert = (scale * grad_rows).astype(jnp.bfloat16)
        grad_act = jnp.dot(grad_expert, down_w.T, preferred_element_type=jnp.float32)
        grad_gate = (grad_act * pre_up * sigmoid_gate * (1.0 + pre_gate * (1.0 - sigmoid_gate))).astype(jnp.bfloat16)
        grad_up = (grad_act * pre_gate * sigmoid_gate).astype(jnp.bfloat16)
        grad_part = (jnp.dot(grad_gate, gate_w.T, preferred_element_type=jnp.float32) + jnp.dot(grad_up, up_w.T, preferred_element_type=jnp.float32)).astype(jnp.bfloat16)
        grad_sum = grad_sum.at[rows_tok].add(grad_part.astype(jnp.float32))
        return ((routed_sum, grad_sum, weight_grad), None)
    start = (jnp.zeros((TOKENS + 1, D), jnp.float32), jnp.zeros((TOKENS + 1, D), jnp.float32), jnp.zeros((TOKENS + 1, TOP), jnp.float32))
    (routed_sum, grad_sum, weight_grad), _ = lax.scan(one_expert, start, (w_gate, w_up, w_down, source_tok, source_k))
    grad_normed = grad_sum[:TOKENS]
    scaled = grad_normed * gain
    grad_tokens = (inv_rms * scaled - tokens_f * inv_rms ** 3 * lax.optimization_barrier(jnp.mean(tokens_f * scaled, axis=1, keepdims=True))).astype(jnp.bfloat16)
    return (routed_sum[:TOKENS].astype(jnp.bfloat16), grad_tokens, weight_grad[:TOKENS])
```

```python
import jax
import jax.numpy as jnp
from jax import lax
from jax.sharding import PartitionSpec as P

EPS = 1e-06
BF = jnp.bfloat16
F32 = jnp.float32


def contract_last(left, right):
    return lax.dot_general(left, right, (((1,), (1,)), ((), ())), preferred_element_type=F32)


def contract_first(left, right):
    return lax.dot_general(left, right, (((0,), (0,)), ((), ())), preferred_element_type=F32)


def rounded(value):
    return lax.reduce_precision(value, exponent_bits=8, mantissa_bits=7)


def pieces(value):
    high = rounded(value)
    middle = rounded(value - high)
    return high, middle, value - high - middle


def packed(columns):
    rows = columns[0].shape[0]
    parts = [piece for column in columns for piece in pieces(column)]
    lane = lax.broadcasted_iota(jnp.int32, (rows, 128), 1)
    result = jnp.zeros((rows, 128), F32)
    for at, part in enumerate(parts):
        result = jnp.where(lane == at, part, result)
    return result.astype(BF)


def unpacked(block, at):
    block = block.astype(F32)
    return block[:, 3 * at : 3 * at + 1] + block[:, 3 * at + 1 : 3 * at + 2] + block[:, 3 * at + 2 : 3 * at + 3]


def exchange(rows, devices, cap_src):
    blocked = rows.reshape(devices, cap_src, rows.shape[1])
    moved = lax.all_to_all(blocked, ("tp", "ep"), split_axis=0, concat_axis=0, tiled=True)
    return moved.reshape(rows.shape)


def local(tokens, gain, routes, route_weights, w_gate, w_up, w_down, grad_out):
    tok_dev, half_dim = tokens.shape
    top_k = routes.shape[1]
    section_size = lax.axis_size("section")
    full_dim = half_dim * section_size
    experts = lax.axis_size("tp") * lax.axis_size("ep")
    cap_src = max(2, tok_dev * top_k // experts + 1)
    slots = experts * cap_src
    gate_mat, up_mat, down_mat = (w_gate[0], w_up[0], w_down[0])
    ff_dim = gate_mat.shape[1]
    swap = [(i, (i + 1) % section_size) for i in range(section_size)]

    routes_t = routes.T
    weights_t = route_weights.T
    slot = lax.broadcasted_iota(jnp.int32, (slots, tok_dev), 0)
    expert_of, rank_of = slot // cap_src, slot % cap_src
    named = [routes_t[k : k + 1, :] == expert_of for k in range(top_k)]
    member = sum(n.astype(F32) for n in named)
    earlier = lax.broadcasted_iota(jnp.int32, (tok_dev, tok_dev), 0) < lax.broadcasted_iota(
        jnp.int32, (tok_dev, tok_dev), 1
    )
    rank = jnp.dot(member.astype(BF), earlier.astype(BF), preferred_element_type=F32)
    at_rank = rank == rank_of.astype(F32)
    picked = jnp.where(at_rank, member, 0.0)
    select = picked.astype(BF)
    weighted = sum(
        jnp.where(named[k] & at_rank, weights_t[k : k + 1, :], 0.0) for k in range(top_k)
    )
    slot_weight = jnp.sum(weighted, axis=1, keepdims=True)

    outgoing = jnp.dot(select, tokens, preferred_element_type=F32).astype(BF)
    arrived = exchange(outgoing, experts, cap_src).astype(F32)
    grad_rows = (
        slot_weight * jnp.dot(select, grad_out, preferred_element_type=F32)
    ).astype(BF)
    grad_arrived = exchange(grad_rows, experts, cap_src)

    tokens_f = tokens.astype(F32)
    squares = jnp.sum(tokens_f * tokens_f, axis=1, keepdims=True)
    other_squares = lax.ppermute(squares, "section", swap)
    inv_rms = lax.rsqrt((squares + other_squares) / full_dim + EPS)

    scaled_rows = (arrived * gain).astype(BF)
    slot_squares = jnp.sum(arrived * arrived, axis=1, keepdims=True)
    own_pre = rounded(
        jnp.concatenate(
            [
                jnp.dot(scaled_rows, gate_mat, preferred_element_type=F32),
                jnp.dot(scaled_rows, up_mat, preferred_element_type=F32),
            ],
            axis=1,
        )
    )
    other_pre = lax.ppermute(
        jnp.concatenate([own_pre.astype(BF), packed([slot_squares])], axis=1), "section", swap
    )
    raw_pre = own_pre + other_pre[:, : 2 * ff_dim].astype(F32)
    slot_total = slot_squares + unpacked(other_pre[:, 2 * ff_dim :], 0)
    slot_inv = lax.rsqrt(slot_total / full_dim + EPS)
    raw_gate, raw_up = raw_pre[:, :ff_dim], raw_pre[:, ff_dim:]
    pre_gate, pre_up = raw_gate * slot_inv, raw_up * slot_inv
    sigmoid_gate = jax.nn.sigmoid(pre_gate)
    activated = (pre_gate * sigmoid_gate * pre_up).astype(BF)
    expert_out = jnp.dot(activated, down_mat, preferred_element_type=F32).astype(BF)
    returned = exchange(expert_out, experts, cap_src)

    own_act = rounded(contract_last(grad_arrived, down_mat))
    grad_act = own_act + lax.ppermute(own_act.astype(BF), "section", swap).astype(F32)
    grad_gate = (grad_act * pre_up * sigmoid_gate * (1.0 + pre_gate * (1.0 - sigmoid_gate))).astype(BF)
    grad_up = (grad_act * pre_gate * sigmoid_gate).astype(BF)
    weight_dot = jnp.sum(activated.astype(F32) * grad_act, axis=1, keepdims=True)
    mean_dot = jnp.sum(
        grad_gate.astype(F32) * raw_gate + grad_up.astype(F32) * raw_up, axis=1, keepdims=True
    )
    grad_part = (contract_last(grad_gate, gate_mat) + contract_last(grad_up, up_mat)).astype(BF)
    back = exchange(
        jnp.concatenate([grad_part, packed([weight_dot, mean_dot])], axis=1), experts, cap_src
    )

    weight_high = rounded(weighted)
    weight_low = weighted - weight_high
    halves = contract_first(
        jnp.concatenate([weight_high, weight_low], axis=1).astype(BF), returned
    )
    routed = (halves[:tok_dev] + halves[tok_dev:]).astype(BF)

    summed = contract_first(select, back)
    mean_total = unpacked(summed[:, half_dim:], 1)
    slot_dot = unpacked(back[:, half_dim:], 0)
    grad_weights = (
        jnp.stack(
            [
                jnp.sum(jnp.where(named[k] & at_rank, slot_dot, 0.0), axis=0)
                for k in range(top_k)
            ],
            axis=1,
        )
        / route_weights
    )
    scaled = summed[:, :half_dim] * gain
    grad_tokens = (inv_rms * scaled - tokens_f * inv_rms**3 * (mean_total / full_dim)).astype(BF)
    return (routed, grad_tokens, grad_weights)


def solution(mesh):
    return jax.shard_map(
        local,
        mesh=mesh,
        in_specs=(
            P(("tp", "ep"), "section"),
            P("section"),
            P(("tp", "ep"), None),
            P(("tp", "ep"), None),
            P(("tp", "ep"), "section", None),
            P(("tp", "ep"), "section", None),
            P(("tp", "ep"), None, "section"),
            P(("tp", "ep"), "section"),
        ),
        out_specs=(P(("tp", "ep"), "section"), P(("tp", "ep"), "section"), P(("tp", "ep"), None)),
        check_vma=False,
    )
```

```python
import jax
import jax.numpy as jnp
from jax import lax
from jax.experimental import pallas as pl
from jax.experimental.pallas import tpu as pltpu
from jax.sharding import PartitionSpec as P

EPS = 1e-06
BF = jnp.bfloat16
F32 = jnp.float32


def contract_last(left, right):
    return lax.dot_general(left, right, (((1,), (1,)), ((), ())), preferred_element_type=F32)


def contract_first(left, right):
    return lax.dot_general(left, right, (((0,), (0,)), ((), ())), preferred_element_type=F32)


SMALL = pl.CostEstimate(flops=1, bytes_accessed=1, transcendentals=0)
ROOM = pltpu.CompilerParams(vmem_limit_bytes=40 * 1024 * 1024)


def act_kernel(rows_ref, down_ref, out_ref):
    out_ref[...] = contract_last(rows_ref[...], down_ref[...]).astype(BF)


def grad_act_part(rows, down_mat):
    slots, half_dim = rows.shape
    ff_dim = down_mat.shape[0]
    block = 256
    return pl.pallas_call(
        act_kernel,
        grid=(ff_dim // block,),
        in_specs=[
            pl.BlockSpec((slots, half_dim), lambda i: (0, 0)),
            pl.BlockSpec((block, half_dim), lambda i: (i, 0)),
        ],
        out_specs=pl.BlockSpec((slots, block), lambda i: (0, i)),
        out_shape=jax.ShapeDtypeStruct((slots, ff_dim), BF),
        compiler_params=ROOM,
        cost_estimate=SMALL,
        name="grad_act",
    )(rows, down_mat)


def in_pieces(value):
    high = value.astype(BF).astype(F32)
    middle = (value - high).astype(BF).astype(F32)
    return high, middle, value - high - middle


def part_kernel(
    pre_a, pre_b, act_a, act_b, done_ref, gate_ref, up_ref, out_ref, gate_grad, up_grad
):
    ff_dim = act_a.shape[1]
    half_dim = done_ref.shape[1]
    block = gate_ref.shape[0]
    step = pl.program_id(0)

    @pl.when(step == 0)
    def _():
        pre_gate = pre_a[:, :ff_dim].astype(F32) + pre_b[:, :ff_dim].astype(F32)
        pre_up = pre_a[:, ff_dim:].astype(F32) + pre_b[:, ff_dim:].astype(F32)
        grad_act = act_a[...].astype(F32) + act_b[...].astype(F32)
        sigmoid_gate = jax.nn.sigmoid(pre_gate)
        activated = (pre_gate * sigmoid_gate * pre_up).astype(BF)
        by_gate = grad_act * pre_up * sigmoid_gate * (1.0 + pre_gate * (1.0 - sigmoid_gate))
        by_up = grad_act * pre_gate * sigmoid_gate
        gate_grad[...] = by_gate.astype(BF)
        up_grad[...] = by_up.astype(BF)
        weight_dot = jnp.sum(activated.astype(F32) * grad_act, axis=1, keepdims=True)
        mean_dot = jnp.sum(by_gate * pre_gate + by_up * pre_up, axis=1, keepdims=True)
        lane = lax.broadcasted_iota(jnp.int32, (done_ref.shape[0], 128), 1)
        sums = jnp.zeros(lane.shape, F32)
        for at, part in enumerate(in_pieces(weight_dot) + in_pieces(mean_dot)):
            sums = jnp.where(lane == at, part, sums)
        out_ref[:, 2 * half_dim :] = sums.astype(BF)
        out_ref[:, :half_dim] = done_ref[...]

    columns = pl.ds(pl.multiple_of(half_dim + step * block, 128), block)
    out_ref[:, columns] = (
        contract_last(gate_grad[...], gate_ref[...]) + contract_last(up_grad[...], up_ref[...])
    ).astype(BF)


def grad_parts(own_pre, other_pre, own_act, other_act, expert_out, gate_mat, up_mat):
    slots, ff_dim = own_act.shape
    half_dim = gate_mat.shape[0]
    block = 512
    whole = lambda width: pl.BlockSpec((slots, width), lambda i: (0, 0))
    weights = pl.BlockSpec((block, ff_dim), lambda i: (i, 0))
    return pl.pallas_call(
        part_kernel,
        grid=(half_dim // block,),
        in_specs=[whole(2 * ff_dim)] * 2 + [whole(ff_dim)] * 2 + [whole(half_dim)] + [weights] * 2,
        out_specs=whole(2 * half_dim + 128),
        out_shape=jax.ShapeDtypeStruct((slots, 2 * half_dim + 128), BF),
        scratch_shapes=[pltpu.VMEM((slots, ff_dim), BF)] * 2,
        compiler_params=ROOM,
        cost_estimate=SMALL,
        name="grad_parts",
    )(own_pre, other_pre, own_act, other_act, expert_out, gate_mat, up_mat)


def rounded(value):
    return lax.reduce_precision(value, exponent_bits=8, mantissa_bits=7)


def unpacked(block, at):
    block = block.astype(F32)
    return block[:, 3 * at : 3 * at + 1] + block[:, 3 * at + 1 : 3 * at + 2] + block[:, 3 * at + 2 : 3 * at + 3]


def blocks(rows, devices):
    return rows.reshape(devices, rows.shape[0] // devices, rows.shape[1])


def exchange(blocked):
    return lax.all_to_all(blocked, ("tp", "ep"), split_axis=0, concat_axis=0, tiled=True)


def local(tokens, gain, routes, route_weights, w_gate, w_up, w_down, grad_out):
    tok_dev, half_dim = tokens.shape
    top_k = routes.shape[1]
    section_size = lax.axis_size("section")
    full_dim = half_dim * section_size
    experts = lax.axis_size("tp") * lax.axis_size("ep")
    cap_src = max(2, tok_dev * top_k // experts + 1)
    slots = experts * cap_src
    gate_mat, up_mat, down_mat = (w_gate[0], w_up[0], w_down[0])
    ff_dim = gate_mat.shape[1]
    swap = [(i, (i + 1) % section_size) for i in range(section_size)]

    routes_t = routes.T
    weights_t = route_weights.T
    slot = lax.broadcasted_iota(jnp.int32, (slots, tok_dev), 0)
    expert_of, rank_of = slot // cap_src, slot % cap_src
    named = [routes_t[k : k + 1, :] == expert_of for k in range(top_k)]
    member = sum(n.astype(F32) for n in named)
    earlier = lax.broadcasted_iota(jnp.int32, (tok_dev, tok_dev), 0) < lax.broadcasted_iota(
        jnp.int32, (tok_dev, tok_dev), 1
    )
    rank = jnp.dot(member.astype(BF), earlier.astype(BF), preferred_element_type=F32)
    at_rank = rank == rank_of.astype(F32)
    picked = jnp.where(at_rank, member, 0.0)
    select = picked.astype(BF)
    weighted = sum(
        jnp.where(named[k] & at_rank, weights_t[k : k + 1, :], 0.0) for k in range(top_k)
    )
    slot_weight = jnp.sum(weighted, axis=1, keepdims=True)

    tokens_f = tokens.astype(F32)
    squares = jnp.sum(tokens_f * tokens_f, axis=1, keepdims=True)
    inv_rms = lax.rsqrt((squares + lax.ppermute(squares, "section", swap)) / full_dim + EPS)
    normed = (tokens_f * inv_rms * gain).astype(BF)
    outgoing = jnp.dot(select, normed, preferred_element_type=F32).astype(BF)
    arrived = exchange(blocks(outgoing, experts)).reshape(slots, half_dim)
    grad_rows = (
        slot_weight * jnp.dot(select, grad_out, preferred_element_type=F32)
    ).astype(BF)
    grad_blocks = exchange(blocks(grad_rows, experts))

    own_pre = rounded(
        jnp.concatenate(
            [
                jnp.dot(arrived, gate_mat, preferred_element_type=F32),
                jnp.dot(arrived, up_mat, preferred_element_type=F32),
            ],
            axis=1,
        )
    )
    pre_send = own_pre.astype(BF)
    other_pre = lax.ppermute(pre_send, "section", swap)
    pre = own_pre + other_pre.astype(F32)
    pre_gate, pre_up = pre[:, :ff_dim], pre[:, ff_dim:]
    sigmoid_gate = jax.nn.sigmoid(pre_gate)
    activated = lax.optimization_barrier((pre_gate * sigmoid_gate * pre_up).astype(BF))
    expert_out = jnp.dot(activated, down_mat, preferred_element_type=F32).astype(BF)
    grad_arrived = grad_blocks.reshape(slots, half_dim)
    own_act = grad_act_part(grad_arrived, down_mat)
    other_act = lax.ppermute(own_act, "section", swap)
    parts = grad_parts(pre_send, other_pre, own_act, other_act, expert_out, gate_mat, up_mat)
    back = exchange(blocks(parts, experts)).reshape(parts.shape)
    returned, back = back[:, :half_dim], back[:, half_dim:]

    weight_high = rounded(weighted)
    weight_low = weighted - weight_high
    halves = contract_first(
        jnp.concatenate([weight_high, weight_low], axis=1).astype(BF), returned
    )
    routed = (halves[:tok_dev] + halves[tok_dev:]).astype(BF)

    summed = contract_first(select, back)
    mean_total = unpacked(summed[:, half_dim:], 1) / inv_rms
    slot_dot = unpacked(back[:, half_dim:], 0)
    grad_weights = (
        jnp.stack(
            [
                jnp.sum(jnp.where(named[k] & at_rank, slot_dot, 0.0), axis=0)
                for k in range(top_k)
            ],
            axis=1,
        )
        / route_weights
    )
    scaled = summed[:, :half_dim] * gain
    grad_tokens = (inv_rms * scaled - tokens_f * inv_rms**3 * (mean_total / full_dim)).astype(BF)
    return (routed, grad_tokens, grad_weights)


def solution(mesh):
    return jax.shard_map(
        local,
        mesh=mesh,
        in_specs=(
            P(("tp", "ep"), "section"),
            P("section"),
            P(("tp", "ep"), None),
            P(("tp", "ep"), None),
            P(("tp", "ep"), "section", None),
            P(("tp", "ep"), "section", None),
            P(("tp", "ep"), None, "section"),
            P(("tp", "ep"), "section"),
        ),
        out_specs=(P(("tp", "ep"), "section"), P(("tp", "ep"), "section"), P(("tp", "ep"), None)),
        check_vma=False,
    )
```

```python
import jax
import jax.numpy as jnp
from jax import lax
from jax.experimental import pallas as pl
from jax.experimental.pallas import tpu as pltpu
from jax.sharding import PartitionSpec as P

EPS = 1e-06
BF = jnp.bfloat16
F32 = jnp.float32


def contract_last(left, right):
    return lax.dot_general(left, right, (((1,), (1,)), ((), ())), preferred_element_type=F32)


def contract_first(left, right):
    return lax.dot_general(left, right, (((0,), (0,)), ((), ())), preferred_element_type=F32)


SMALL = pl.CostEstimate(flops=1, bytes_accessed=1, transcendentals=0)


def room(mib):
    return pltpu.CompilerParams(vmem_limit_bytes=mib * 1024 * 1024)


def column_block(width):
    return 512 if width % 512 == 0 else width


def send_kernel(select_ref, tokens_ref, inv_ref, gain_ref, out_ref):
    normed = (tokens_ref[...].astype(F32) * inv_ref[...] * gain_ref[...]).astype(BF)
    rows = jnp.dot(select_ref[...], normed, preferred_element_type=F32).astype(BF)
    out_ref[...] = rows.reshape(out_ref.shape)


def token_messages(select, tokens, inv_rms, gain, peers):
    tok_dev, half_dim = tokens.shape
    slots = select.shape[0]
    block = column_block(half_dim)
    return pl.pallas_call(
        send_kernel,
        grid=(half_dim // block,),
        in_specs=[
            pl.BlockSpec((slots, tok_dev), lambda i: (0, 0)),
            pl.BlockSpec((tok_dev, block), lambda i: (0, i)),
            pl.BlockSpec((tok_dev, 1), lambda i: (0, 0)),
            pl.BlockSpec((1, block), lambda i: (0, i)),
        ],
        out_specs=pl.BlockSpec((peers, slots // peers, block), lambda i: (0, 0, i)),
        out_shape=jax.ShapeDtypeStruct((peers, slots // peers, half_dim), BF),
        compiler_params=room(16),
        cost_estimate=SMALL,
        name="token_messages",
    )(select, tokens, inv_rms, gain.reshape(1, half_dim))


def act_kernel(rows_ref, down_ref, out_ref, kept):
    @pl.when(pl.program_id(0) == 0)
    def _():
        kept[...] = rows_ref[...].reshape(kept.shape)

    out_ref[...] = contract_last(kept[...], down_ref[...]).astype(BF)


def grad_act_part(rows, down_mat):
    peers, per_peer, half_dim = rows.shape
    slots = peers * per_peer
    ff_dim = down_mat.shape[0]
    block = ff_dim // 3
    return pl.pallas_call(
        act_kernel,
        grid=(3,),
        in_specs=[
            pl.BlockSpec((peers, per_peer, half_dim), lambda i: (0, 0, 0)),
            pl.BlockSpec((block, half_dim), lambda i: (i, 0)),
        ],
        out_specs=pl.BlockSpec((slots, block), lambda i: (0, i)),
        out_shape=jax.ShapeDtypeStruct((slots, ff_dim), BF),
        scratch_shapes=[pltpu.VMEM((slots, half_dim), BF)],
        compiler_params=room(24),
        cost_estimate=SMALL,
        name="grad_act",
    )(rows, down_mat)


def in_pieces(value):
    high = value.astype(BF).astype(F32)
    middle = (value - high).astype(BF).astype(F32)
    return high, middle, value - high - middle


def part_kernel(
    top_k, pre_a, pre_b, act_a, act_b, done_ref, gate_ref, up_ref, out_ref, gate_grad, up_grad
):
    ff_dim = act_a.shape[1]
    half_dim = done_ref.shape[1]
    block = gate_ref.shape[0]
    peers, per_peer, _ = out_ref.shape
    step = pl.program_id(0)

    @pl.when(step == 0)
    def _():
        pre_gate = pre_a[:, :ff_dim].astype(F32) + pre_b[:, :ff_dim].astype(F32)
        pre_up = pre_a[:, ff_dim:].astype(F32) + pre_b[:, ff_dim:].astype(F32)
        grad_act = act_a[...].astype(F32) + act_b[...].astype(F32)
        sigmoid_gate = jax.nn.sigmoid(pre_gate)
        activated = (pre_gate * sigmoid_gate * pre_up).astype(BF)
        by_gate = grad_act * pre_up * sigmoid_gate * (1.0 + pre_gate * (1.0 - sigmoid_gate))
        by_up = grad_act * pre_gate * sigmoid_gate
        gate_grad[...] = by_gate.astype(BF)
        up_grad[...] = by_up.astype(BF)
        weight_dot = jnp.sum(activated.astype(F32) * grad_act, axis=1, keepdims=True)
        mean_dot = jnp.sum(by_gate * pre_gate + by_up * pre_up, axis=1, keepdims=True)
        lane = lax.broadcasted_iota(jnp.int32, (done_ref.shape[0], 128), 1)
        sums = jnp.zeros(lane.shape, F32)
        for at, part in enumerate(in_pieces(weight_dot) + in_pieces(mean_dot)):
            sums = jnp.where((lane >= at * top_k) & (lane < (at + 1) * top_k), part, sums)
        out_ref[:, :, 2 * half_dim :] = sums.astype(BF).reshape(peers, per_peer, 128)
        out_ref[:, :, :half_dim] = done_ref[...].reshape(peers, per_peer, half_dim)

    columns = pl.ds(pl.multiple_of(half_dim + step * block, 128), block)
    part = contract_last(gate_grad[...], gate_ref[...]) + contract_last(up_grad[...], up_ref[...])
    out_ref[:, :, columns] = part.astype(BF).reshape(peers, per_peer, block)


def grad_parts(own_pre, other_pre, own_act, other_act, expert_out, gate_mat, up_mat, peers, top_k):
    slots, ff_dim = own_act.shape
    half_dim = gate_mat.shape[0]
    block = column_block(half_dim)
    shape = (peers, slots // peers, 2 * half_dim + 128)
    whole = lambda width: pl.BlockSpec((slots, width), lambda i: (0, 0))
    weights = pl.BlockSpec((block, ff_dim), lambda i: (i, 0))

    def body(*refs):
        part_kernel(top_k, *refs)

    return pl.pallas_call(
        body,
        grid=(half_dim // block,),
        in_specs=[whole(2 * ff_dim)] * 2 + [whole(ff_dim)] * 2 + [whole(half_dim)] + [weights] * 2,
        out_specs=pl.BlockSpec(shape, lambda i: (0, 0, 0)),
        out_shape=jax.ShapeDtypeStruct(shape, BF),
        scratch_shapes=[pltpu.VMEM((slots, ff_dim), BF)] * 2,
        compiler_params=room(40),
        cost_estimate=SMALL,
        name="grad_parts",
    )(own_pre, other_pre, own_act, other_act, expert_out, gate_mat, up_mat)


def finish_kernel(
    top_k,
    full_dim,
    out_rows,
    grad_rows,
    sum_rows,
    weights_ref,
    select_ref,
    slot_k_ref,
    inv_ref,
    tokens_ref,
    gain_ref,
    routed_ref,
    grad_ref,
    slot_ref,
    mean_ref,
):
    tok_dev = inv_ref.shape[0]
    slots = select_ref.shape[1]

    @pl.when(pl.program_id(0) == 0)
    def _():
        lane = lax.broadcasted_iota(jnp.int32, (slots, 128), 1)
        sums = sum_rows[...].reshape(slots, 128).astype(F32)
        sums = jnp.where((lane % top_k).astype(F32) == slot_k_ref[...], sums, 0.0).astype(BF)
        tail = jnp.dot(select_ref[...], sums, preferred_element_type=F32)
        slot_ref[...] = tail
        at = lax.broadcasted_iota(jnp.int32, tail.shape, 1)
        mean = jnp.where((at >= 3 * top_k) & (at < 6 * top_k), tail, 0.0)
        mean = jnp.sum(mean, axis=1, keepdims=True) / inv_ref[...] / full_dim
        mean_ref[...] = jnp.broadcast_to(mean, mean_ref.shape)

    outs = out_rows[...].reshape(slots, routed_ref.shape[1])
    halves = jnp.dot(weights_ref[...], outs, preferred_element_type=F32)
    routed_ref[...] = (halves[:tok_dev] + halves[tok_dev:]).astype(BF)
    grads = grad_rows[...].reshape(slots, routed_ref.shape[1])
    scaled = jnp.dot(select_ref[...], grads, preferred_element_type=F32) * gain_ref[...]
    inv = inv_ref[...]
    drop = tokens_ref[...].astype(F32) * (inv * inv * inv) * mean_ref[:, :1]
    grad_ref[...] = (inv * scaled - drop).astype(BF)


def finish(back, weights_t, select_t, slot_k, inv_rms, tokens, gain, top_k, full_dim):
    peers, per_peer, _ = back.shape
    tok_dev, half_dim = tokens.shape
    slots = peers * per_peer
    block = column_block(half_dim)
    steps = half_dim // block
    fixed = lambda shape: pl.BlockSpec(shape, lambda i: (0, 0))
    moving = lambda rows: pl.BlockSpec((rows, block), lambda i: (0, i))

    def body(*refs):
        finish_kernel(top_k, full_dim, *refs)

    return pl.pallas_call(
        body,
        grid=(steps,),
        in_specs=[
            pl.BlockSpec((peers, per_peer, block), lambda i: (0, 0, i)),
            pl.BlockSpec((peers, per_peer, block), lambda i: (0, 0, steps + i)),
            pl.BlockSpec((peers, per_peer, 128), lambda i: (0, 0, 2 * half_dim // 128)),
            fixed((2 * tok_dev, slots)),
            fixed((tok_dev, slots)),
            fixed((slots, 1)),
            fixed((tok_dev, 1)),
            moving(tok_dev),
            moving(1),
        ],
        out_specs=[moving(tok_dev), moving(tok_dev), fixed((tok_dev, 128))],
        out_shape=[
            jax.ShapeDtypeStruct((tok_dev, half_dim), BF),
            jax.ShapeDtypeStruct((tok_dev, half_dim), BF),
            jax.ShapeDtypeStruct((tok_dev, 128), F32),
        ],
        scratch_shapes=[pltpu.VMEM((tok_dev, 128), F32)],
        compiler_params=room(16),
        cost_estimate=SMALL,
        name="finish",
    )(back, back, back, weights_t, select_t, slot_k, inv_rms, tokens, gain.reshape(1, half_dim))


def rounded(value):
    return lax.reduce_precision(value, exponent_bits=8, mantissa_bits=7)


def blocks(rows, devices):
    return rows.reshape(devices, rows.shape[0] // devices, rows.shape[1])


def exchange(blocked):
    return lax.all_to_all(blocked, ("tp", "ep"), split_axis=0, concat_axis=0, tiled=True)


def local(tokens, gain, routes, route_weights, w_gate, w_up, w_down, grad_out):
    tok_dev, half_dim = tokens.shape
    top_k = routes.shape[1]
    section_size = lax.axis_size("section")
    full_dim = half_dim * section_size
    experts = lax.axis_size("tp") * lax.axis_size("ep")
    cap_src = max(2, tok_dev * top_k // experts + 1)
    slots = experts * cap_src
    gate_mat, up_mat, down_mat = (w_gate[0], w_up[0], w_down[0])
    ff_dim = gate_mat.shape[1]
    swap = [(i, (i + 1) % section_size) for i in range(section_size)]

    routes_t = routes.T
    weights_t = route_weights.T
    slot = lax.broadcasted_iota(jnp.int32, (slots, tok_dev), 0)
    expert_of, rank_of = slot // cap_src, slot % cap_src
    named = [routes_t[k : k + 1, :] == expert_of for k in range(top_k)]
    member = sum(n.astype(F32) for n in named)
    earlier = lax.broadcasted_iota(jnp.int32, (tok_dev, tok_dev), 0) < lax.broadcasted_iota(
        jnp.int32, (tok_dev, tok_dev), 1
    )
    rank = jnp.dot(member.astype(BF), earlier.astype(BF), preferred_element_type=F32)
    at_rank = rank == rank_of.astype(F32)
    picked = jnp.where(at_rank, member, 0.0)
    select = picked.astype(BF)
    weighted = sum(
        jnp.where(named[k] & at_rank, weights_t[k : k + 1, :], 0.0) for k in range(top_k)
    )
    slot_weight = jnp.sum(weighted, axis=1, keepdims=True)

    tokens_f = tokens.astype(F32)
    squares = jnp.sum(tokens_f * tokens_f, axis=1, keepdims=True)
    inv_rms = lax.rsqrt((squares + lax.ppermute(squares, "section", swap)) / full_dim + EPS)
    arrived = exchange(token_messages(select, tokens, inv_rms, gain, experts)).reshape(slots, half_dim)
    grad_rows = (
        slot_weight * jnp.dot(select, grad_out, preferred_element_type=F32)
    ).astype(BF)
    grad_blocks = exchange(blocks(grad_rows, experts))

    own_pre = rounded(
        jnp.concatenate(
            [
                jnp.dot(arrived, gate_mat, preferred_element_type=F32),
                jnp.dot(arrived, up_mat, preferred_element_type=F32),
            ],
            axis=1,
        )
    )
    pre_send = own_pre.astype(BF)
    other_pre = lax.ppermute(pre_send, "section", swap)
    pre = own_pre + other_pre.astype(F32)
    pre_gate, pre_up = pre[:, :ff_dim], pre[:, ff_dim:]
    sigmoid_gate = jax.nn.sigmoid(pre_gate)
    activated = lax.optimization_barrier((pre_gate * sigmoid_gate * pre_up).astype(BF))
    expert_out = jnp.dot(activated, down_mat, preferred_element_type=F32).astype(BF)
    own_act = grad_act_part(grad_blocks, down_mat)
    other_act = lax.ppermute(own_act, "section", swap)
    parts = grad_parts(
        pre_send, other_pre, own_act, other_act, expert_out, gate_mat, up_mat, experts, top_k
    )
    back = exchange(parts)

    weight_high = rounded(weighted)
    weight_low = weighted - weight_high
    slot_k = jnp.sum(
        sum(jnp.where(n & at_rank, float(k), 0.0) for k, n in enumerate(named)),
        axis=1,
        keepdims=True,
    )
    weights_both = jnp.concatenate([weight_high, weight_low], axis=1).astype(BF).T
    routed, grad_tokens, tail = finish(
        back, weights_both, select.T, slot_k, inv_rms, tokens, gain, top_k, full_dim
    )
    slot_dot = tail[:, :top_k] + tail[:, top_k : 2 * top_k] + tail[:, 2 * top_k : 3 * top_k]
    grad_weights = slot_dot / route_weights
    return (routed, grad_tokens, grad_weights)


def solution(mesh):
    return jax.shard_map(
        local,
        mesh=mesh,
        in_specs=(
            P(("tp", "ep"), "section"),
            P("section"),
            P(("tp", "ep"), None),
            P(("tp", "ep"), None),
            P(("tp", "ep"), "section", None),
            P(("tp", "ep"), "section", None),
            P(("tp", "ep"), None, "section"),
            P(("tp", "ep"), "section"),
        ),
        out_specs=(P(("tp", "ep"), "section"), P(("tp", "ep"), "section"), P(("tp", "ep"), None)),
        check_vma=False,
    )
```

```python
import jax
import jax.numpy as jnp
from jax import lax
from jax.experimental import pallas as pl
from jax.experimental.pallas import tpu as pltpu
from jax.sharding import Mesh, PartitionSpec as P

EPS = 1e-06
BF = jnp.bfloat16
F32 = jnp.float32
CORES = 2


def contract_last(left, right):
    return lax.dot_general(left, right, (((1,), (1,)), ((), ())), preferred_element_type=F32)


def contract_first(left, right):
    return lax.dot_general(left, right, (((0,), (0,)), ((), ())), preferred_element_type=F32)


SMALL = pl.CostEstimate(flops=1, bytes_accessed=1, transcendentals=0)


def room(mib):
    return pltpu.CompilerParams(vmem_limit_bytes=mib * 1024 * 1024)


def column_block(width):
    return 512 if width % 512 == 0 else width


def send_kernel(select_ref, own_ref, mate_ref, own_inv, mate_inv, gain_ref, out_ref):
    tok_dev = own_ref.shape[0]
    own = (own_ref[...].astype(F32) * own_inv[...] * gain_ref[...]).astype(BF)
    mate = (mate_ref[...].astype(F32) * mate_inv[...] * gain_ref[...]).astype(BF)
    rows = jnp.dot(select_ref[:, :tok_dev], own, preferred_element_type=F32)
    rows += jnp.dot(select_ref[:, tok_dev:], mate, preferred_element_type=F32)
    out_ref[...] = rows.astype(BF).reshape(out_ref.shape)


def token_messages(select, tokens, mate_tokens, inv_rms, mate_inv, gain, chips):
    tok_dev, half_dim = tokens.shape
    slots = select.shape[0]
    block = half_dim // 2
    moving = lambda rows: pl.BlockSpec((rows, block), lambda i: (0, i))
    column = pl.BlockSpec((tok_dev, 1), lambda i: (0, 0))
    return pl.pallas_call(
        send_kernel,
        grid=(half_dim // block,),
        in_specs=[
            pl.BlockSpec((slots, CORES * tok_dev), lambda i: (0, 0)),
            moving(tok_dev),
            moving(tok_dev),
            column,
            column,
            moving(1),
        ],
        out_specs=pl.BlockSpec((chips, slots // chips, block), lambda i: (0, 0, i)),
        out_shape=jax.ShapeDtypeStruct((chips, slots // chips, half_dim), BF),
        compiler_params=room(16),
        cost_estimate=SMALL,
        name="token_messages",
    )(select, tokens, mate_tokens, inv_rms, mate_inv, gain.reshape(1, half_dim))


def act_kernel(rows_ref, down_ref, out_ref, kept):
    @pl.when(pl.program_id(0) == 0)
    def _():
        kept[...] = rows_ref[...].reshape(kept.shape)

    out_ref[...] = contract_last(kept[...], down_ref[...]).astype(BF)


def grad_act_part(rows, down_mat):
    peers, per_peer, half_dim = rows.shape
    slots = peers * per_peer
    ff_dim = down_mat.shape[0]
    block = ff_dim // 3
    return pl.pallas_call(
        act_kernel,
        grid=(3,),
        in_specs=[
            pl.BlockSpec((peers, per_peer, half_dim), lambda i: (0, 0, 0)),
            pl.BlockSpec((block, half_dim), lambda i: (i, 0)),
        ],
        out_specs=pl.BlockSpec((slots, block), lambda i: (0, i)),
        out_shape=jax.ShapeDtypeStruct((slots, ff_dim), BF),
        scratch_shapes=[pltpu.VMEM((slots, half_dim), BF)],
        compiler_params=room(24),
        cost_estimate=SMALL,
        name="grad_act",
    )(rows, down_mat)


def in_pieces(value):
    high = value.astype(BF).astype(F32)
    middle = (value - high).astype(BF).astype(F32)
    return high, middle, value - high - middle


def part_kernel(
    top_k, pre_a, pre_b, act_a, act_b, done_ref, gate_ref, up_ref, out_ref, gate_grad, up_grad
):
    ff_dim = act_a.shape[1]
    half_dim = done_ref.shape[1]
    block = gate_ref.shape[0]
    peers, per_peer, _ = out_ref.shape
    step = pl.program_id(0)

    @pl.when(step == 0)
    def _():
        pre_gate = pre_a[:, :ff_dim].astype(F32) + pre_b[:, :ff_dim].astype(F32)
        pre_up = pre_a[:, ff_dim:].astype(F32) + pre_b[:, ff_dim:].astype(F32)
        grad_act = act_a[...].astype(F32) + act_b[...].astype(F32)
        sigmoid_gate = jax.nn.sigmoid(pre_gate)
        activated = (pre_gate * sigmoid_gate * pre_up).astype(BF)
        by_gate = grad_act * pre_up * sigmoid_gate * (1.0 + pre_gate * (1.0 - sigmoid_gate))
        by_up = grad_act * pre_gate * sigmoid_gate
        gate_grad[...] = by_gate.astype(BF)
        up_grad[...] = by_up.astype(BF)
        weight_dot = jnp.sum(activated.astype(F32) * grad_act, axis=1, keepdims=True)
        mean_dot = jnp.sum(by_gate * pre_gate + by_up * pre_up, axis=1, keepdims=True)
        lane = lax.broadcasted_iota(jnp.int32, (done_ref.shape[0], 128), 1)
        sums = jnp.zeros(lane.shape, F32)
        for at, part in enumerate(in_pieces(weight_dot) + in_pieces(mean_dot)):
            sums = jnp.where((lane >= at * top_k) & (lane < (at + 1) * top_k), part, sums)
        out_ref[:, :, 2 * half_dim :] = sums.astype(BF).reshape(peers, per_peer, 128)
        out_ref[:, :, :half_dim] = done_ref[...].reshape(peers, per_peer, half_dim)

    columns = pl.ds(pl.multiple_of(half_dim + step * block, 128), block)
    part = contract_last(gate_grad[...], gate_ref[...]) + contract_last(up_grad[...], up_ref[...])
    out_ref[:, :, columns] = part.astype(BF).reshape(peers, per_peer, block)


def grad_parts(own_pre, other_pre, own_act, other_act, expert_out, gate_mat, up_mat, peers, top_k):
    slots, ff_dim = own_act.shape
    half_dim = gate_mat.shape[0]
    block = column_block(half_dim)
    shape = (peers, slots // peers, 2 * half_dim + 128)
    whole = lambda width: pl.BlockSpec((slots, width), lambda i: (0, 0))
    weights = pl.BlockSpec((block, ff_dim), lambda i: (i, 0))

    def body(*refs):
        part_kernel(top_k, *refs)

    return pl.pallas_call(
        body,
        grid=(half_dim // block,),
        in_specs=[whole(2 * ff_dim)] * 2 + [whole(ff_dim)] * 2 + [whole(half_dim)] + [weights] * 2,
        out_specs=pl.BlockSpec(shape, lambda i: (0, 0, 0)),
        out_shape=jax.ShapeDtypeStruct(shape, BF),
        scratch_shapes=[pltpu.VMEM((slots, ff_dim), BF)] * 2,
        compiler_params=room(40),
        cost_estimate=SMALL,
        name="grad_parts",
    )(own_pre, other_pre, own_act, other_act, expert_out, gate_mat, up_mat)


def finish_kernel(
    top_k,
    full_dim,
    out_rows,
    grad_rows,
    sum_rows,
    weights_ref,
    select_ref,
    slot_k_ref,
    inv_ref,
    tokens_ref,
    gain_ref,
    routed_ref,
    grad_ref,
    slot_ref,
    mean_ref,
):
    tok_dev = inv_ref.shape[0]
    slots = select_ref.shape[1]

    @pl.when(pl.program_id(0) == 0)
    def _():
        lane = lax.broadcasted_iota(jnp.int32, (slots, 128), 1)
        sums = sum_rows[...].reshape(slots, 128).astype(F32)
        sums = jnp.where((lane % top_k).astype(F32) == slot_k_ref[...], sums, 0.0).astype(BF)
        tail = jnp.dot(select_ref[...], sums, preferred_element_type=F32)
        slot_ref[...] = tail
        at = lax.broadcasted_iota(jnp.int32, tail.shape, 1)
        mean = jnp.where((at >= 3 * top_k) & (at < 6 * top_k), tail, 0.0)
        mean = jnp.sum(mean, axis=1, keepdims=True) / inv_ref[...] / full_dim
        mean_ref[...] = jnp.broadcast_to(mean, mean_ref.shape)

    outs = out_rows[...].reshape(slots, routed_ref.shape[1])
    halves = jnp.dot(weights_ref[...], outs, preferred_element_type=F32)
    routed_ref[...] = (halves[:tok_dev] + halves[tok_dev:]).astype(BF)
    grads = grad_rows[...].reshape(slots, routed_ref.shape[1])
    scaled = jnp.dot(select_ref[...], grads, preferred_element_type=F32) * gain_ref[...]
    inv = inv_ref[...]
    drop = tokens_ref[...].astype(F32) * (inv * inv * inv) * mean_ref[:, :1]
    grad_ref[...] = (inv * scaled - drop).astype(BF)


def finish(back, weights_t, select_t, slot_k, inv_rms, tokens, gain, top_k, full_dim):
    peers, per_peer, _ = back.shape
    tok_dev, half_dim = tokens.shape
    slots = peers * per_peer
    block = column_block(half_dim)
    steps = half_dim // block
    fixed = lambda shape: pl.BlockSpec(shape, lambda i: (0, 0))
    moving = lambda rows: pl.BlockSpec((rows, block), lambda i: (0, i))

    def body(*refs):
        finish_kernel(top_k, full_dim, *refs)

    return pl.pallas_call(
        body,
        grid=(steps,),
        in_specs=[
            pl.BlockSpec((peers, per_peer, block), lambda i: (0, 0, i)),
            pl.BlockSpec((peers, per_peer, block), lambda i: (0, 0, steps + i)),
            pl.BlockSpec((peers, per_peer, 128), lambda i: (0, 0, 2 * half_dim // 128)),
            fixed((2 * tok_dev, slots)),
            fixed((tok_dev, slots)),
            fixed((slots, 1)),
            fixed((tok_dev, 1)),
            moving(tok_dev),
            moving(1),
        ],
        out_specs=[moving(tok_dev), moving(tok_dev), fixed((tok_dev, 128))],
        out_shape=[
            jax.ShapeDtypeStruct((tok_dev, half_dim), BF),
            jax.ShapeDtypeStruct((tok_dev, half_dim), BF),
            jax.ShapeDtypeStruct((tok_dev, 128), F32),
        ],
        scratch_shapes=[pltpu.VMEM((tok_dev, 128), F32)],
        compiler_params=room(16),
        cost_estimate=SMALL,
        name="finish",
    )(back, back, back, weights_t, select_t, slot_k, inv_rms, tokens, gain.reshape(1, half_dim))


def rounded(value):
    return lax.reduce_precision(value, exponent_bits=8, mantissa_bits=7)


def blocks(rows, devices):
    return rows.reshape(devices, rows.shape[0] // devices, rows.shape[1])


def exchange(blocked, axes):
    return lax.all_to_all(blocked, axes, split_axis=0, concat_axis=0, tiled=True)


def local(tokens, gain, routes, route_weights, w_gate, w_up, w_down, grad_out):
    tok_dev, half_dim = tokens.shape
    top_k = routes.shape[1]
    section_size = lax.axis_size("section")
    full_dim = half_dim * section_size
    experts = lax.axis_size("tp") * lax.axis_size("zy") * CORES
    cap_src = max(2, tok_dev * top_k // experts + 1)
    slots = experts * cap_src
    gate_mat, up_mat, down_mat = (w_gate[0], w_up[0], w_down[0])
    ff_dim = gate_mat.shape[1]
    swap = [(i, (i + 1) % section_size) for i in range(section_size)]

    routes_t = routes.T
    weights_t = route_weights.T
    slot = lax.broadcasted_iota(jnp.int32, (slots, tok_dev), 0)
    expert_of, rank_of = slot // cap_src, slot % cap_src
    named = [routes_t[k : k + 1, :] == expert_of for k in range(top_k)]
    member = sum(n.astype(F32) for n in named)
    earlier = lax.broadcasted_iota(jnp.int32, (tok_dev, tok_dev), 0) < lax.broadcasted_iota(
        jnp.int32, (tok_dev, tok_dev), 1
    )
    rank = jnp.dot(member.astype(BF), earlier.astype(BF), preferred_element_type=F32)
    at_rank = rank == rank_of.astype(F32)
    picked = jnp.where(at_rank, member, 0.0)
    select = picked.astype(BF)
    weighted = sum(
        jnp.where(named[k] & at_rank, weights_t[k : k + 1, :], 0.0) for k in range(top_k)
    )

    flip = [(0, 1), (1, 0)]
    core = lax.axis_index("core")
    chips = experts // CORES
    pair = CORES * tok_dev
    tokens_f = tokens.astype(F32)
    squares = jnp.sum(tokens_f * tokens_f, axis=1, keepdims=True)
    other_squares = lax.ppermute(squares, "section", swap)
    mate_tokens = lax.ppermute(tokens, "core", flip)
    mate_other = lax.ppermute(squares, ("section", "core"), [(i, 3 - i) for i in range(4)])
    facts = jnp.concatenate([routes.astype(F32), route_weights], axis=1)
    mate_facts = lax.ppermute(facts, "core", flip)
    mate_grad = lax.ppermute(grad_out, "core", flip)
    mate_f = mate_tokens.astype(F32)
    mate_squares = jnp.sum(mate_f * mate_f, axis=1, keepdims=True)
    inv_rms = lax.rsqrt((squares + other_squares) / full_dim + EPS)
    mate_inv = lax.rsqrt((mate_squares + mate_other) / full_dim + EPS)

    facts_t = jnp.concatenate([facts, mate_facts], axis=0).T
    row = lax.broadcasted_iota(jnp.int32, (slots, pair), 0)
    column = lax.broadcasted_iota(jnp.int32, (slots, pair), 1)
    wanted = (row // (CORES * cap_src) * CORES + core).astype(F32)
    here = row // cap_src % CORES == (column // tok_dev + core) % CORES
    pair_named = [(facts_t[k : k + 1, :] == wanted) & here for k in range(top_k)]
    pair_member = sum(n.astype(F32) for n in pair_named)
    before = lax.broadcasted_iota(jnp.int32, (pair, pair), 0)
    after = lax.broadcasted_iota(jnp.int32, (pair, pair), 1)
    pair_earlier = (before // tok_dev == after // tok_dev) & (before < after)
    pair_rank = jnp.dot(
        pair_member.astype(BF), pair_earlier.astype(BF), preferred_element_type=F32
    )
    pair_at = pair_rank == (row % cap_src).astype(F32)
    pair_select = jnp.where(pair_at, pair_member, 0.0).astype(BF)
    pair_weighted = sum(
        jnp.where(n & pair_at, facts_t[top_k + k : top_k + k + 1, :], 0.0)
        for k, n in enumerate(pair_named)
    )
    slot_weight = jnp.sum(pair_weighted, axis=1, keepdims=True)

    between = ("tp", "zy")
    messages = token_messages(pair_select, tokens, mate_tokens, inv_rms, mate_inv, gain, chips)
    arrived = exchange(messages, between).reshape(slots, half_dim)
    grad_pair = jnp.concatenate([grad_out, mate_grad], axis=0)
    grad_rows = (
        slot_weight * jnp.dot(pair_select, grad_pair, preferred_element_type=F32)
    ).astype(BF)
    grad_blocks = exchange(blocks(grad_rows, chips), between)

    own_pre = rounded(
        jnp.concatenate(
            [
                jnp.dot(arrived, gate_mat, preferred_element_type=F32),
                jnp.dot(arrived, up_mat, preferred_element_type=F32),
            ],
            axis=1,
        )
    )
    pre_send = own_pre.astype(BF)
    other_pre = lax.ppermute(pre_send, "section", swap)
    pre = own_pre + other_pre.astype(F32)
    pre_gate, pre_up = pre[:, :ff_dim], pre[:, ff_dim:]
    sigmoid_gate = jax.nn.sigmoid(pre_gate)
    activated = lax.optimization_barrier((pre_gate * sigmoid_gate * pre_up).astype(BF))
    expert_out = jnp.dot(activated, down_mat, preferred_element_type=F32).astype(BF)
    own_act = grad_act_part(grad_blocks, down_mat)
    other_act = lax.ppermute(own_act, "section", swap)
    parts = grad_parts(
        pre_send, other_pre, own_act, other_act, expert_out, gate_mat, up_mat, experts, top_k
    )
    back = exchange(parts, ("tp", "zy", "core"))

    weight_high = rounded(weighted)
    weight_low = weighted - weight_high
    slot_k = jnp.sum(
        sum(jnp.where(n & at_rank, float(k), 0.0) for k, n in enumerate(named)),
        axis=1,
        keepdims=True,
    )
    weights_both = jnp.concatenate([weight_high, weight_low], axis=1).astype(BF).T
    routed, grad_tokens, tail = finish(
        back, weights_both, select.T, slot_k, inv_rms, tokens, gain, top_k, full_dim
    )
    slot_dot = tail[:, :top_k] + tail[:, top_k : 2 * top_k] + tail[:, 2 * top_k : 3 * top_k]
    grad_weights = slot_dot / route_weights
    return (routed, grad_tokens, grad_weights)


def solution(mesh):
    sizes = mesh.shape
    shape = (sizes["section"], sizes["tp"], sizes["ep"] // CORES, CORES)
    fine = Mesh(mesh.devices.reshape(shape), ("section", "tp", "zy", "core"))
    rows = ("tp", "zy", "core")
    return jax.shard_map(
        local,
        mesh=fine,
        in_specs=(
            P(rows, "section"),
            P("section"),
            P(rows, None),
            P(rows, None),
            P(rows, "section", None),
            P(rows, "section", None),
            P(rows, None, "section"),
            P(rows, "section"),
        ),
        out_specs=(P(rows, "section"), P(rows, "section"), P(rows, None)),
        check_vma=False,
    )
```

```python
import jax
import jax.numpy as jnp
from jax import lax
from jax.experimental import pallas as pl
from jax.experimental.pallas import tpu as pltpu
from jax.sharding import Mesh, PartitionSpec as P

EPS = 1e-06
BF = jnp.bfloat16
F32 = jnp.float32
CORES = 2


def contract_last(left, right):
    return lax.dot_general(left, right, (((1,), (1,)), ((), ())), preferred_element_type=F32)


def contract_first(left, right):
    return lax.dot_general(left, right, (((0,), (0,)), ((), ())), preferred_element_type=F32)


SMALL = pl.CostEstimate(flops=1, bytes_accessed=1, transcendentals=0)


def room(mib):
    return pltpu.CompilerParams(vmem_limit_bytes=mib * 1024 * 1024)


def column_block(width):
    return 512 if width % 512 == 0 else width


def send_kernel(select_ref, own_ref, mate_ref, own_inv, mate_inv, gain_ref, out_ref):
    tok_dev = own_ref.shape[0]
    own = (own_ref[...].astype(F32) * own_inv[...] * gain_ref[...]).astype(BF)
    mate = (mate_ref[...].astype(F32) * mate_inv[...] * gain_ref[...]).astype(BF)
    rows = jnp.dot(select_ref[:, :tok_dev], own, preferred_element_type=F32)
    rows += jnp.dot(select_ref[:, tok_dev:], mate, preferred_element_type=F32)
    out_ref[...] = rows.astype(BF).reshape(out_ref.shape)


def token_messages(select, tokens, mate_tokens, inv_rms, mate_inv, gain, chips):
    tok_dev, half_dim = tokens.shape
    slots = select.shape[0]
    block = half_dim // 2
    moving = lambda rows: pl.BlockSpec((rows, block), lambda i: (0, i))
    column = pl.BlockSpec((tok_dev, 1), lambda i: (0, 0))
    return pl.pallas_call(
        send_kernel,
        grid=(half_dim // block,),
        in_specs=[
            pl.BlockSpec((slots, CORES * tok_dev), lambda i: (0, 0)),
            moving(tok_dev),
            moving(tok_dev),
            column,
            column,
            moving(1),
        ],
        out_specs=pl.BlockSpec((chips, slots // chips, block), lambda i: (0, 0, i)),
        out_shape=jax.ShapeDtypeStruct((chips, slots // chips, half_dim), BF),
        compiler_params=room(16),
        cost_estimate=SMALL,
        name="token_messages",
    )(select, tokens, mate_tokens, inv_rms, mate_inv, gain.reshape(1, half_dim))


def act_kernel(rows_ref, down_ref, out_ref, kept):
    @pl.when(pl.program_id(0) == 0)
    def _():
        kept[...] = rows_ref[...].reshape(kept.shape)

    out_ref[...] = contract_last(kept[...], down_ref[...]).astype(BF)


def grad_act_part(rows, down_mat):
    peers, per_peer, half_dim = rows.shape
    slots = peers * per_peer
    ff_dim = down_mat.shape[0]
    block = ff_dim // 3
    return pl.pallas_call(
        act_kernel,
        grid=(3,),
        in_specs=[
            pl.BlockSpec((peers, per_peer, half_dim), lambda i: (0, 0, 0)),
            pl.BlockSpec((block, half_dim), lambda i: (i, 0)),
        ],
        out_specs=pl.BlockSpec((slots, block), lambda i: (0, i)),
        out_shape=jax.ShapeDtypeStruct((slots, ff_dim), BF),
        scratch_shapes=[pltpu.VMEM((slots, half_dim), BF)],
        compiler_params=room(24),
        cost_estimate=SMALL,
        name="grad_act",
    )(rows, down_mat)


def in_pieces(value):
    high = value.astype(BF).astype(F32)
    middle = (value - high).astype(BF).astype(F32)
    return high, middle, value - high - middle


def part_kernel(
    top_k, pre_a, pre_b, act_a, act_b, done_ref, gate_ref, up_ref, out_ref, gate_grad, up_grad
):
    ff_dim = act_a.shape[1]
    half_dim = done_ref.shape[1]
    block = gate_ref.shape[0]
    peers, per_peer, _ = out_ref.shape
    step = pl.program_id(0)

    @pl.when(step == 0)
    def _():
        pre_gate = pre_a[:, :ff_dim].astype(F32) + pre_b[:, :ff_dim].astype(F32)
        pre_up = pre_a[:, ff_dim:].astype(F32) + pre_b[:, ff_dim:].astype(F32)
        grad_act = act_a[...].astype(F32) + act_b[...].astype(F32)
        sigmoid_gate = jax.nn.sigmoid(pre_gate)
        activated = (pre_gate * sigmoid_gate * pre_up).astype(BF)
        by_gate = grad_act * pre_up * sigmoid_gate * (1.0 + pre_gate * (1.0 - sigmoid_gate))
        by_up = grad_act * pre_gate * sigmoid_gate
        gate_grad[...] = by_gate.astype(BF)
        up_grad[...] = by_up.astype(BF)
        weight_dot = jnp.sum(activated.astype(F32) * grad_act, axis=1, keepdims=True)
        mean_dot = jnp.sum(by_gate * pre_gate + by_up * pre_up, axis=1, keepdims=True)
        lane = lax.broadcasted_iota(jnp.int32, (done_ref.shape[0], 128), 1)
        sums = jnp.zeros(lane.shape, F32)
        for at, part in enumerate(in_pieces(weight_dot) + in_pieces(mean_dot)):
            sums = jnp.where((lane >= at * top_k) & (lane < (at + 1) * top_k), part, sums)
        out_ref[:, :, 2 * half_dim :] = sums.astype(BF).reshape(peers, per_peer, 128)
        out_ref[:, :, :half_dim] = done_ref[...].reshape(peers, per_peer, half_dim)

    columns = pl.ds(pl.multiple_of(half_dim + step * block, 128), block)
    part = contract_last(gate_grad[...], gate_ref[...]) + contract_last(up_grad[...], up_ref[...])
    out_ref[:, :, columns] = part.astype(BF).reshape(peers, per_peer, block)


def grad_parts(own_pre, other_pre, own_act, other_act, expert_out, gate_mat, up_mat, peers, top_k):
    slots, ff_dim = own_act.shape
    half_dim = gate_mat.shape[0]
    block = column_block(half_dim)
    shape = (peers, slots // peers, 2 * half_dim + 128)
    whole = lambda width: pl.BlockSpec((slots, width), lambda i: (0, 0))
    weights = pl.BlockSpec((block, ff_dim), lambda i: (i, 0))

    def body(*refs):
        part_kernel(top_k, *refs)

    return pl.pallas_call(
        body,
        grid=(half_dim // block,),
        in_specs=[whole(2 * ff_dim)] * 2 + [whole(ff_dim)] * 2 + [whole(half_dim)] + [weights] * 2,
        out_specs=pl.BlockSpec(shape, lambda i: (0, 0, 0)),
        out_shape=jax.ShapeDtypeStruct(shape, BF),
        scratch_shapes=[pltpu.VMEM((slots, ff_dim), BF)] * 2,
        compiler_params=room(40),
        cost_estimate=SMALL,
        name="grad_parts",
    )(own_pre, other_pre, own_act, other_act, expert_out, gate_mat, up_mat)


def finish_kernel(
    top_k,
    full_dim,
    out_rows,
    grad_rows,
    sum_rows,
    weights_ref,
    select_ref,
    slot_k_ref,
    inv_ref,
    tokens_ref,
    gain_ref,
    routed_ref,
    grad_ref,
    slot_ref,
    mean_ref,
):
    tok_dev = inv_ref.shape[0]
    slots = select_ref.shape[1]

    @pl.when(pl.program_id(0) == 0)
    def _():
        lane = lax.broadcasted_iota(jnp.int32, (slots, 128), 1)
        sums = sum_rows[...].reshape(slots, 128).astype(F32)
        sums = jnp.where((lane % top_k).astype(F32) == slot_k_ref[...], sums, 0.0).astype(BF)
        tail = jnp.dot(select_ref[...], sums, preferred_element_type=F32)
        slot_ref[...] = tail
        at = lax.broadcasted_iota(jnp.int32, tail.shape, 1)
        mean = jnp.where((at >= 3 * top_k) & (at < 6 * top_k), tail, 0.0)
        mean = jnp.sum(mean, axis=1, keepdims=True) / inv_ref[...] / full_dim
        mean_ref[...] = jnp.broadcast_to(mean, mean_ref.shape)

    outs = out_rows[...].reshape(slots, routed_ref.shape[1])
    halves = jnp.dot(weights_ref[...], outs, preferred_element_type=F32)
    routed_ref[...] = (halves[:tok_dev] + halves[tok_dev:]).astype(BF)
    grads = grad_rows[...].reshape(slots, routed_ref.shape[1])
    scaled = jnp.dot(select_ref[...], grads, preferred_element_type=F32) * gain_ref[...]
    inv = inv_ref[...]
    drop = tokens_ref[...].astype(F32) * (inv * inv * inv) * mean_ref[:, :1]
    grad_ref[...] = (inv * scaled - drop).astype(BF)


def finish(back, weights_t, select_t, slot_k, inv_rms, tokens, gain, top_k, full_dim):
    peers, per_peer, _ = back.shape
    tok_dev, half_dim = tokens.shape
    slots = peers * per_peer
    block = column_block(half_dim)
    steps = half_dim // block
    fixed = lambda shape: pl.BlockSpec(shape, lambda i: (0, 0))
    moving = lambda rows: pl.BlockSpec((rows, block), lambda i: (0, i))

    def body(*refs):
        finish_kernel(top_k, full_dim, *refs)

    return pl.pallas_call(
        body,
        grid=(steps,),
        in_specs=[
            pl.BlockSpec((peers, per_peer, block), lambda i: (0, 0, i)),
            pl.BlockSpec((peers, per_peer, block), lambda i: (0, 0, steps + i)),
            pl.BlockSpec((peers, per_peer, 128), lambda i: (0, 0, 2 * half_dim // 128)),
            fixed((2 * tok_dev, slots)),
            fixed((tok_dev, slots)),
            fixed((slots, 1)),
            fixed((tok_dev, 1)),
            moving(tok_dev),
            moving(1),
        ],
        out_specs=[moving(tok_dev), moving(tok_dev), fixed((tok_dev, 128))],
        out_shape=[
            jax.ShapeDtypeStruct((tok_dev, half_dim), BF),
            jax.ShapeDtypeStruct((tok_dev, half_dim), BF),
            jax.ShapeDtypeStruct((tok_dev, 128), F32),
        ],
        scratch_shapes=[pltpu.VMEM((tok_dev, 128), F32)],
        compiler_params=room(16),
        cost_estimate=SMALL,
        name="finish",
    )(back, back, back, weights_t, select_t, slot_k, inv_rms, tokens, gain.reshape(1, half_dim))


def rounded(value):
    return lax.reduce_precision(value, exponent_bits=8, mantissa_bits=7)


def blocks(rows, devices):
    return rows.reshape(devices, rows.shape[0] // devices, rows.shape[1])


def exchange(blocked, axes):
    return lax.all_to_all(blocked, axes, split_axis=0, concat_axis=0, tiled=True)


def local(tokens, gain, routes, route_weights, w_gate, w_up, w_down, grad_out):
    tok_dev, half_dim = tokens.shape
    top_k = routes.shape[1]
    section_size = lax.axis_size("section")
    full_dim = half_dim * section_size
    experts = lax.axis_size("tp") * lax.axis_size("zy") * CORES
    cap_src = max(2, tok_dev * top_k // experts + 1)
    slots = experts * cap_src
    gate_mat, up_mat, down_mat = (w_gate[0], w_up[0], w_down[0])
    ff_dim = gate_mat.shape[1]
    swap = [(i, (i + 1) % section_size) for i in range(section_size)]

    flip = [(0, 1), (1, 0)]
    mate_routes = lax.ppermute(routes, "core", flip)
    routes_t = routes.T
    weights_t = route_weights.T
    slot = lax.broadcasted_iota(jnp.int32, (slots, tok_dev), 0)
    expert_of, rank_of = slot // cap_src, slot % cap_src
    named = [routes_t[k : k + 1, :] == expert_of for k in range(top_k)]
    member = sum(n.astype(F32) for n in named)
    earlier = lax.broadcasted_iota(jnp.int32, (tok_dev, tok_dev), 0) < lax.broadcasted_iota(
        jnp.int32, (tok_dev, tok_dev), 1
    )
    rank = jnp.dot(member.astype(BF), earlier.astype(BF), preferred_element_type=F32)
    at_rank = rank == rank_of.astype(F32)
    picked = jnp.where(at_rank, member, 0.0)
    select = picked.astype(BF)
    weighted = sum(
        jnp.where(named[k] & at_rank, weights_t[k : k + 1, :], 0.0) for k in range(top_k)
    )

    core = lax.axis_index("core")
    chips = experts // CORES
    pair = CORES * tok_dev
    tokens_f = tokens.astype(F32)
    squares = jnp.sum(tokens_f * tokens_f, axis=1, keepdims=True)
    other_squares = lax.ppermute(squares, "section", swap)
    mate_tokens = lax.ppermute(tokens, "core", flip)
    mate_other = lax.ppermute(squares, ("section", "core"), [(i, 3 - i) for i in range(4)])
    mate_weights = lax.ppermute(route_weights, "core", flip)
    mate_grad = lax.ppermute(grad_out, "core", flip)
    mate_f = mate_tokens.astype(F32)
    mate_squares = jnp.sum(mate_f * mate_f, axis=1, keepdims=True)
    inv_rms = lax.rsqrt((squares + other_squares) / full_dim + EPS)
    mate_inv = lax.rsqrt((mate_squares + mate_other) / full_dim + EPS)

    pair_routes = jnp.concatenate([routes_t, mate_routes.T], axis=1)
    pair_weights = jnp.concatenate([weights_t, mate_weights.T], axis=1)
    row = lax.broadcasted_iota(jnp.int32, (slots, pair), 0)
    column = lax.broadcasted_iota(jnp.int32, (slots, pair), 1)
    wanted = row // (CORES * cap_src) * CORES + core
    here = row // cap_src % CORES == (column // tok_dev + core) % CORES
    pair_named = [(pair_routes[k : k + 1, :] == wanted) & here for k in range(top_k)]
    pair_member = sum(n.astype(F32) for n in pair_named)
    before = lax.broadcasted_iota(jnp.int32, (pair, pair), 0)
    after = lax.broadcasted_iota(jnp.int32, (pair, pair), 1)
    pair_earlier = (before // tok_dev == after // tok_dev) & (before < after)
    pair_rank = jnp.dot(
        pair_member.astype(BF), pair_earlier.astype(BF), preferred_element_type=F32
    )
    pair_at = pair_rank == (row % cap_src).astype(F32)
    pair_select = jnp.where(pair_at, pair_member, 0.0).astype(BF)
    pair_weighted = sum(
        jnp.where(n & pair_at, pair_weights[k : k + 1, :], 0.0)
        for k, n in enumerate(pair_named)
    )
    slot_weight = jnp.sum(pair_weighted, axis=1, keepdims=True)

    between = ("tp", "zy")
    messages = token_messages(pair_select, tokens, mate_tokens, inv_rms, mate_inv, gain, chips)
    arrived = exchange(messages, between).reshape(slots, half_dim)
    grad_pair = jnp.concatenate([grad_out, mate_grad], axis=0)
    grad_rows = (
        slot_weight * jnp.dot(pair_select, grad_pair, preferred_element_type=F32)
    ).astype(BF)
    grad_blocks = exchange(blocks(grad_rows, chips), between)

    own_pre = rounded(
        jnp.concatenate(
            [
                jnp.dot(arrived, gate_mat, preferred_element_type=F32),
                jnp.dot(arrived, up_mat, preferred_element_type=F32),
            ],
            axis=1,
        )
    )
    pre_send = own_pre.astype(BF)
    other_pre = lax.ppermute(pre_send, "section", swap)
    pre = own_pre + other_pre.astype(F32)
    pre_gate, pre_up = pre[:, :ff_dim], pre[:, ff_dim:]
    sigmoid_gate = jax.nn.sigmoid(pre_gate)
    activated = lax.optimization_barrier((pre_gate * sigmoid_gate * pre_up).astype(BF))
    expert_out = jnp.dot(activated, down_mat, preferred_element_type=F32).astype(BF)
    own_act = grad_act_part(grad_blocks, down_mat)
    other_act = lax.ppermute(own_act, "section", swap)
    parts = grad_parts(
        pre_send, other_pre, own_act, other_act, expert_out, gate_mat, up_mat, experts, top_k
    )
    back = exchange(parts, ("tp", "zy", "core"))

    weight_high = rounded(weighted)
    weight_low = weighted - weight_high
    slot_k = jnp.sum(
        sum(jnp.where(n & at_rank, float(k), 0.0) for k, n in enumerate(named)),
        axis=1,
        keepdims=True,
    )
    weights_both = jnp.concatenate([weight_high, weight_low], axis=1).astype(BF).T
    routed, grad_tokens, tail = finish(
        back, weights_both, select.T, slot_k, inv_rms, tokens, gain, top_k, full_dim
    )
    slot_dot = tail[:, :top_k] + tail[:, top_k : 2 * top_k] + tail[:, 2 * top_k : 3 * top_k]
    grad_weights = slot_dot / route_weights
    return (routed, grad_tokens, grad_weights)


def solution(mesh):
    sizes = mesh.shape
    shape = (sizes["section"], sizes["tp"], sizes["ep"] // CORES, CORES)
    fine = Mesh(mesh.devices.reshape(shape), ("section", "tp", "zy", "core"))
    rows = ("tp", "zy", "core")
    return jax.shard_map(
        local,
        mesh=fine,
        in_specs=(
            P(rows, "section"),
            P("section"),
            P(rows, None),
            P(rows, None),
            P(rows, "section", None),
            P(rows, "section", None),
            P(rows, None, "section"),
            P(rows, "section"),
        ),
        out_specs=(P(rows, "section"), P(rows, "section"), P(rows, None)),
        check_vma=False,
    )
```

```python
import jax
import jax.numpy as jnp
from jax import lax
from jax.experimental import pallas as pl
from jax.experimental.pallas import tpu as pltpu
from jax.sharding import Mesh, PartitionSpec as P

EPS = 1e-06
BF = jnp.bfloat16
F32 = jnp.float32
CORES = 2


def contract_last(left, right):
    return lax.dot_general(left, right, (((1,), (1,)), ((), ())), preferred_element_type=F32)


def contract_first(left, right):
    return lax.dot_general(left, right, (((0,), (0,)), ((), ())), preferred_element_type=F32)


SMALL = pl.CostEstimate(flops=1, bytes_accessed=1, transcendentals=0)


def room(mib):
    return pltpu.CompilerParams(vmem_limit_bytes=mib * 1024 * 1024)


def column_block(width):
    return width // 2 if width % 256 == 0 else width


def send_kernel(select_ref, own_ref, mate_ref, own_inv, mate_inv, gain_ref, out_ref):
    tok_dev = own_ref.shape[0]
    own = (own_ref[...].astype(F32) * own_inv[...] * gain_ref[...]).astype(BF)
    mate = (mate_ref[...].astype(F32) * mate_inv[...] * gain_ref[...]).astype(BF)
    rows = jnp.dot(select_ref[:, :tok_dev], own, preferred_element_type=F32)
    rows += jnp.dot(select_ref[:, tok_dev:], mate, preferred_element_type=F32)
    out_ref[...] = rows.astype(BF).reshape(out_ref.shape)


def token_messages(select, tokens, mate_tokens, inv_rms, mate_inv, gain, chips):
    tok_dev, half_dim = tokens.shape
    slots = select.shape[0]
    block = half_dim // 2
    moving = lambda rows: pl.BlockSpec((rows, block), lambda i: (0, i))
    column = pl.BlockSpec((tok_dev, 1), lambda i: (0, 0))
    return pl.pallas_call(
        send_kernel,
        grid=(half_dim // block,),
        in_specs=[
            pl.BlockSpec((slots, CORES * tok_dev), lambda i: (0, 0)),
            moving(tok_dev),
            moving(tok_dev),
            column,
            column,
            moving(1),
        ],
        out_specs=pl.BlockSpec((chips, slots // chips, block), lambda i: (0, 0, i)),
        out_shape=jax.ShapeDtypeStruct((chips, slots // chips, half_dim), BF),
        compiler_params=room(16),
        cost_estimate=SMALL,
        name="token_messages",
    )(select, tokens, mate_tokens, inv_rms, mate_inv, gain.reshape(1, half_dim))


def act_kernel(rows_ref, down_ref, out_ref, kept):
    @pl.when(pl.program_id(0) == 0)
    def _():
        kept[...] = rows_ref[...].reshape(kept.shape)

    out_ref[...] = contract_last(kept[...], down_ref[...]).astype(BF)


def grad_act_part(rows, down_mat):
    peers, per_peer, half_dim = rows.shape
    slots = peers * per_peer
    ff_dim = down_mat.shape[0]
    block = ff_dim // 3
    return pl.pallas_call(
        act_kernel,
        grid=(3,),
        in_specs=[
            pl.BlockSpec((peers, per_peer, half_dim), lambda i: (0, 0, 0)),
            pl.BlockSpec((block, half_dim), lambda i: (i, 0)),
        ],
        out_specs=pl.BlockSpec((slots, block), lambda i: (0, i)),
        out_shape=jax.ShapeDtypeStruct((slots, ff_dim), BF),
        scratch_shapes=[pltpu.VMEM((slots, half_dim), BF)],
        compiler_params=room(24),
        cost_estimate=SMALL,
        name="grad_act",
    )(rows, down_mat)


def in_pieces(value):
    high = value.astype(BF).astype(F32)
    middle = (value - high).astype(BF).astype(F32)
    return high, middle, value - high - middle


def part_kernel(
    top_k, pre_a, pre_b, act_a, act_b, done_ref, gate_ref, up_ref, out_ref, gate_grad, up_grad
):
    ff_dim = act_a.shape[1]
    half_dim = done_ref.shape[1]
    block = gate_ref.shape[0]
    peers, per_peer, _ = out_ref.shape
    step = pl.program_id(0)

    @pl.when(step == 0)
    def _():
        pre_gate = pre_a[:, :ff_dim].astype(F32) + pre_b[:, :ff_dim].astype(F32)
        pre_up = pre_a[:, ff_dim:].astype(F32) + pre_b[:, ff_dim:].astype(F32)
        grad_act = act_a[...].astype(F32) + act_b[...].astype(F32)
        sigmoid_gate = jax.nn.sigmoid(pre_gate)
        activated = (pre_gate * sigmoid_gate * pre_up).astype(BF)
        by_gate = grad_act * pre_up * sigmoid_gate * (1.0 + pre_gate * (1.0 - sigmoid_gate))
        by_up = grad_act * pre_gate * sigmoid_gate
        gate_grad[...] = by_gate.astype(BF)
        up_grad[...] = by_up.astype(BF)
        weight_dot = jnp.sum(activated.astype(F32) * grad_act, axis=1, keepdims=True)
        mean_dot = jnp.sum(by_gate * pre_gate + by_up * pre_up, axis=1, keepdims=True)
        lane = lax.broadcasted_iota(jnp.int32, (done_ref.shape[0], 128), 1)
        sums = jnp.zeros(lane.shape, F32)
        for at, part in enumerate(in_pieces(weight_dot) + in_pieces(mean_dot)):
            sums = jnp.where((lane >= at * top_k) & (lane < (at + 1) * top_k), part, sums)
        out_ref[:, :, 2 * half_dim :] = sums.astype(BF).reshape(peers, per_peer, 128)
        out_ref[:, :, :half_dim] = done_ref[...].reshape(peers, per_peer, half_dim)

    columns = pl.ds(pl.multiple_of(half_dim + step * block, 128), block)
    part = contract_last(gate_grad[...], gate_ref[...]) + contract_last(up_grad[...], up_ref[...])
    out_ref[:, :, columns] = part.astype(BF).reshape(peers, per_peer, block)


def grad_parts(own_pre, other_pre, own_act, other_act, expert_out, gate_mat, up_mat, peers, top_k):
    slots, ff_dim = own_act.shape
    half_dim = gate_mat.shape[0]
    block = column_block(half_dim)
    shape = (peers, slots // peers, 2 * half_dim + 128)
    whole = lambda width: pl.BlockSpec((slots, width), lambda i: (0, 0))
    weights = pl.BlockSpec((block, ff_dim), lambda i: (i, 0))

    def body(*refs):
        part_kernel(top_k, *refs)

    return pl.pallas_call(
        body,
        grid=(half_dim // block,),
        in_specs=[whole(2 * ff_dim)] * 2 + [whole(ff_dim)] * 2 + [whole(half_dim)] + [weights] * 2,
        out_specs=pl.BlockSpec(shape, lambda i: (0, 0, 0)),
        out_shape=jax.ShapeDtypeStruct(shape, BF),
        scratch_shapes=[pltpu.VMEM((slots, ff_dim), BF)] * 2,
        compiler_params=room(40),
        cost_estimate=SMALL,
        name="grad_parts",
    )(own_pre, other_pre, own_act, other_act, expert_out, gate_mat, up_mat)


def finish_kernel(
    top_k,
    full_dim,
    out_rows,
    grad_rows,
    sum_rows,
    weights_ref,
    select_ref,
    slot_k_ref,
    inv_ref,
    tokens_ref,
    gain_ref,
    routed_ref,
    grad_ref,
    slot_ref,
    mean_ref,
):
    tok_dev = inv_ref.shape[0]
    slots = select_ref.shape[1]

    @pl.when(pl.program_id(0) == 0)
    def _():
        lane = lax.broadcasted_iota(jnp.int32, (slots, 128), 1)
        sums = sum_rows[...].reshape(slots, 128).astype(F32)
        sums = jnp.where((lane % top_k).astype(F32) == slot_k_ref[...], sums, 0.0).astype(BF)
        tail = jnp.dot(select_ref[...], sums, preferred_element_type=F32)
        slot_ref[...] = tail
        at = lax.broadcasted_iota(jnp.int32, tail.shape, 1)
        mean = jnp.where((at >= 3 * top_k) & (at < 6 * top_k), tail, 0.0)
        mean = jnp.sum(mean, axis=1, keepdims=True) / inv_ref[...] / full_dim
        mean_ref[...] = jnp.broadcast_to(mean, mean_ref.shape)

    outs = out_rows[...].reshape(slots, routed_ref.shape[1])
    halves = jnp.dot(weights_ref[...], outs, preferred_element_type=F32)
    routed_ref[...] = (halves[:tok_dev] + halves[tok_dev:]).astype(BF)
    grads = grad_rows[...].reshape(slots, routed_ref.shape[1])
    scaled = jnp.dot(select_ref[...], grads, preferred_element_type=F32) * gain_ref[...]
    inv = inv_ref[...]
    drop = tokens_ref[...].astype(F32) * (inv * inv * inv) * mean_ref[:, :1]
    grad_ref[...] = (inv * scaled - drop).astype(BF)


def finish(back, weights_t, select_t, slot_k, inv_rms, tokens, gain, top_k, full_dim):
    peers, per_peer, _ = back.shape
    tok_dev, half_dim = tokens.shape
    slots = peers * per_peer
    block = column_block(half_dim)
    steps = half_dim // block
    fixed = lambda shape: pl.BlockSpec(shape, lambda i: (0, 0))
    moving = lambda rows: pl.BlockSpec((rows, block), lambda i: (0, i))

    def body(*refs):
        finish_kernel(top_k, full_dim, *refs)

    return pl.pallas_call(
        body,
        grid=(steps,),
        in_specs=[
            pl.BlockSpec((peers, per_peer, block), lambda i: (0, 0, i)),
            pl.BlockSpec((peers, per_peer, block), lambda i: (0, 0, steps + i)),
            pl.BlockSpec((peers, per_peer, 128), lambda i: (0, 0, 2 * half_dim // 128)),
            fixed((2 * tok_dev, slots)),
            fixed((tok_dev, slots)),
            fixed((slots, 1)),
            fixed((tok_dev, 1)),
            moving(tok_dev),
            moving(1),
        ],
        out_specs=[moving(tok_dev), moving(tok_dev), fixed((tok_dev, 128))],
        out_shape=[
            jax.ShapeDtypeStruct((tok_dev, half_dim), BF),
            jax.ShapeDtypeStruct((tok_dev, half_dim), BF),
            jax.ShapeDtypeStruct((tok_dev, 128), F32),
        ],
        scratch_shapes=[pltpu.VMEM((tok_dev, 128), F32)],
        compiler_params=room(16),
        cost_estimate=SMALL,
        name="finish",
    )(back, back, back, weights_t, select_t, slot_k, inv_rms, tokens, gain.reshape(1, half_dim))


def rounded(value):
    return lax.reduce_precision(value, exponent_bits=8, mantissa_bits=7)


def blocks(rows, devices):
    return rows.reshape(devices, rows.shape[0] // devices, rows.shape[1])


def exchange(blocked, axes):
    return lax.all_to_all(blocked, axes, split_axis=0, concat_axis=0, tiled=True)


def local(tokens, gain, routes, route_weights, w_gate, w_up, w_down, grad_out):
    tok_dev, half_dim = tokens.shape
    top_k = routes.shape[1]
    section_size = lax.axis_size("section")
    full_dim = half_dim * section_size
    experts = lax.axis_size("tp") * lax.axis_size("zy") * CORES
    cap_src = max(2, tok_dev * top_k // experts + 1)
    slots = experts * cap_src
    gate_mat, up_mat, down_mat = (w_gate[0], w_up[0], w_down[0])
    ff_dim = gate_mat.shape[1]
    swap = [(i, (i + 1) % section_size) for i in range(section_size)]

    flip = [(0, 1), (1, 0)]
    mate_routes = lax.ppermute(routes, "core", flip)
    routes_t = routes.T
    weights_t = route_weights.T
    slot = lax.broadcasted_iota(jnp.int32, (slots, tok_dev), 0)
    expert_of, rank_of = slot // cap_src, slot % cap_src
    named = [routes_t[k : k + 1, :] == expert_of for k in range(top_k)]
    member = sum(n.astype(F32) for n in named)
    earlier = lax.broadcasted_iota(jnp.int32, (tok_dev, tok_dev), 0) < lax.broadcasted_iota(
        jnp.int32, (tok_dev, tok_dev), 1
    )
    rank = jnp.dot(member.astype(BF), earlier.astype(BF), preferred_element_type=F32)
    at_rank = rank == rank_of.astype(F32)
    picked = jnp.where(at_rank, member, 0.0)
    select = picked.astype(BF)
    weighted = sum(
        jnp.where(named[k] & at_rank, weights_t[k : k + 1, :], 0.0) for k in range(top_k)
    )

    core = lax.axis_index("core")
    chips = experts // CORES
    pair = CORES * tok_dev
    tokens_f = tokens.astype(F32)
    squares = jnp.sum(tokens_f * tokens_f, axis=1, keepdims=True)
    other_squares = lax.ppermute(squares, "section", swap)
    mate_tokens = lax.ppermute(tokens, "core", flip)
    mate_other = lax.ppermute(squares, ("section", "core"), [(i, 3 - i) for i in range(4)])
    mate_weights = lax.ppermute(route_weights, "core", flip)
    mate_grad = lax.ppermute(grad_out, "core", flip)
    mate_f = mate_tokens.astype(F32)
    mate_squares = jnp.sum(mate_f * mate_f, axis=1, keepdims=True)
    inv_rms = lax.rsqrt((squares + other_squares) / full_dim + EPS)
    mate_inv = lax.rsqrt((mate_squares + mate_other) / full_dim + EPS)

    pair_routes = jnp.concatenate([routes_t, mate_routes.T], axis=1)
    pair_weights = jnp.concatenate([weights_t, mate_weights.T], axis=1)
    row = lax.broadcasted_iota(jnp.int32, (slots, pair), 0)
    column = lax.broadcasted_iota(jnp.int32, (slots, pair), 1)
    wanted = row // (CORES * cap_src) * CORES + core
    here = row // cap_src % CORES == (column // tok_dev + core) % CORES
    pair_named = [(pair_routes[k : k + 1, :] == wanted) & here for k in range(top_k)]
    pair_member = sum(n.astype(F32) for n in pair_named)
    before = lax.broadcasted_iota(jnp.int32, (pair, pair), 0)
    after = lax.broadcasted_iota(jnp.int32, (pair, pair), 1)
    pair_earlier = (before // tok_dev == after // tok_dev) & (before < after)
    pair_rank = jnp.dot(
        pair_member.astype(BF), pair_earlier.astype(BF), preferred_element_type=F32
    )
    pair_at = pair_rank == (row % cap_src).astype(F32)
    pair_select = jnp.where(pair_at, pair_member, 0.0).astype(BF)
    pair_weighted = sum(
        jnp.where(n & pair_at, pair_weights[k : k + 1, :], 0.0)
        for k, n in enumerate(pair_named)
    )
    slot_weight = jnp.sum(pair_weighted, axis=1, keepdims=True)

    between = ("tp", "zy")
    messages = token_messages(pair_select, tokens, mate_tokens, inv_rms, mate_inv, gain, chips)
    arrived = exchange(messages, between).reshape(slots, half_dim)
    grad_pair = jnp.concatenate([grad_out, mate_grad], axis=0)
    grad_rows = (
        slot_weight * jnp.dot(pair_select, grad_pair, preferred_element_type=F32)
    ).astype(BF)
    grad_blocks = exchange(blocks(grad_rows, chips), between)

    own_pre = rounded(
        jnp.concatenate(
            [
                jnp.dot(arrived, gate_mat, preferred_element_type=F32),
                jnp.dot(arrived, up_mat, preferred_element_type=F32),
            ],
            axis=1,
        )
    )
    pre_send = own_pre.astype(BF)
    other_pre = lax.ppermute(pre_send, "section", swap)
    pre = own_pre + other_pre.astype(F32)
    pre_gate, pre_up = pre[:, :ff_dim], pre[:, ff_dim:]
    sigmoid_gate = jax.nn.sigmoid(pre_gate)
    activated = lax.optimization_barrier((pre_gate * sigmoid_gate * pre_up).astype(BF))
    expert_out = jnp.dot(activated, down_mat, preferred_element_type=F32).astype(BF)
    own_act = grad_act_part(grad_blocks, down_mat)
    other_act = lax.ppermute(own_act, "section", swap)
    parts = grad_parts(
        pre_send, other_pre, own_act, other_act, expert_out, gate_mat, up_mat, experts, top_k
    )
    back = exchange(parts, ("tp", "zy", "core"))

    weight_high = rounded(weighted)
    weight_low = weighted - weight_high
    slot_k = jnp.sum(
        sum(jnp.where(n & at_rank, float(k), 0.0) for k, n in enumerate(named)),
        axis=1,
        keepdims=True,
    )
    weights_both = jnp.concatenate([weight_high, weight_low], axis=1).astype(BF).T
    routed, grad_tokens, tail = finish(
        back, weights_both, select.T, slot_k, inv_rms, tokens, gain, top_k, full_dim
    )
    slot_dot = tail[:, :top_k] + tail[:, top_k : 2 * top_k] + tail[:, 2 * top_k : 3 * top_k]
    grad_weights = slot_dot / route_weights
    return (routed, grad_tokens, grad_weights)


def solution(mesh):
    sizes = mesh.shape
    shape = (sizes["section"], sizes["tp"], sizes["ep"] // CORES, CORES)
    fine = Mesh(mesh.devices.reshape(shape), ("section", "tp", "zy", "core"))
    rows = ("tp", "zy", "core")
    return jax.shard_map(
        local,
        mesh=fine,
        in_specs=(
            P(rows, "section"),
            P("section"),
            P(rows, None),
            P(rows, None),
            P(rows, "section", None),
            P(rows, "section", None),
            P(rows, None, "section"),
            P(rows, "section"),
        ),
        out_specs=(P(rows, "section"), P(rows, "section"), P(rows, None)),
        check_vma=False,
    )
```

```python
import jax
import jax.numpy as jnp
from jax import lax
from jax.experimental import pallas as pl
from jax.experimental.pallas import tpu as pltpu
from jax.sharding import Mesh, PartitionSpec as P

EPS = 1e-06
BF = jnp.bfloat16
F32 = jnp.float32
CORES = 2


def contract_last(left, right):
    return lax.dot_general(left, right, (((1,), (1,)), ((), ())), preferred_element_type=F32)


def contract_first(left, right):
    return lax.dot_general(left, right, (((0,), (0,)), ((), ())), preferred_element_type=F32)


SMALL = pl.CostEstimate(flops=1, bytes_accessed=1, transcendentals=0)


def room(mib):
    return pltpu.CompilerParams(vmem_limit_bytes=mib * 1024 * 1024)


def column_block(width):
    return width // 2 if width % 256 == 0 else width


def send_kernel(select_ref, own_ref, mate_ref, own_inv, mate_inv, gain_ref, out_ref):
    tok_dev = own_ref.shape[0]
    own = (own_ref[...].astype(F32) * own_inv[...] * gain_ref[...]).astype(BF)
    mate = (mate_ref[...].astype(F32) * mate_inv[...] * gain_ref[...]).astype(BF)
    rows = jnp.dot(select_ref[:, :tok_dev], own, preferred_element_type=F32)
    rows += jnp.dot(select_ref[:, tok_dev:], mate, preferred_element_type=F32)
    out_ref[...] = rows.astype(BF).reshape(out_ref.shape)


def token_messages(select, tokens, mate_tokens, inv_rms, mate_inv, gain, chips):
    tok_dev, half_dim = tokens.shape
    slots = select.shape[0]
    block = half_dim // 2
    moving = lambda rows: pl.BlockSpec((rows, block), lambda i: (0, i))
    column = pl.BlockSpec((tok_dev, 1), lambda i: (0, 0))
    return pl.pallas_call(
        send_kernel,
        grid=(half_dim // block,),
        in_specs=[
            pl.BlockSpec((slots, CORES * tok_dev), lambda i: (0, 0)),
            moving(tok_dev),
            moving(tok_dev),
            column,
            column,
            moving(1),
        ],
        out_specs=pl.BlockSpec((chips, slots // chips, block), lambda i: (0, 0, i)),
        out_shape=jax.ShapeDtypeStruct((chips, slots // chips, half_dim), BF),
        compiler_params=room(16),
        cost_estimate=SMALL,
        name="token_messages",
    )(select, tokens, mate_tokens, inv_rms, mate_inv, gain.reshape(1, half_dim))


def act_kernel(rows_ref, down_ref, out_ref, kept):
    @pl.when(pl.program_id(0) == 0)
    def _():
        kept[...] = rows_ref[...].reshape(kept.shape)

    out_ref[...] = contract_last(kept[...], down_ref[...]).astype(BF)


def grad_act_part(rows, down_mat):
    peers, per_peer, half_dim = rows.shape
    slots = peers * per_peer
    ff_dim = down_mat.shape[0]
    block = ff_dim // 2
    return pl.pallas_call(
        act_kernel,
        grid=(2,),
        in_specs=[
            pl.BlockSpec((peers, per_peer, half_dim), lambda i: (0, 0, 0)),
            pl.BlockSpec((block, half_dim), lambda i: (i, 0)),
        ],
        out_specs=pl.BlockSpec((slots, block), lambda i: (0, i)),
        out_shape=jax.ShapeDtypeStruct((slots, ff_dim), BF),
        scratch_shapes=[pltpu.VMEM((slots, half_dim), BF)],
        compiler_params=room(24),
        cost_estimate=SMALL,
        name="grad_act",
    )(rows, down_mat)


def in_pieces(value):
    high = value.astype(BF).astype(F32)
    middle = (value - high).astype(BF).astype(F32)
    return high, middle, value - high - middle


def part_kernel(
    top_k, pre_a, pre_b, act_a, act_b, done_ref, gate_ref, up_ref, out_ref, gate_grad, up_grad
):
    ff_dim = act_a.shape[1]
    half_dim = done_ref.shape[1]
    block = gate_ref.shape[0]
    peers, per_peer, _ = out_ref.shape
    step = pl.program_id(0)

    @pl.when(step == 0)
    def _():
        pre_gate = pre_a[:, :ff_dim].astype(F32) + pre_b[:, :ff_dim].astype(F32)
        pre_up = pre_a[:, ff_dim:].astype(F32) + pre_b[:, ff_dim:].astype(F32)
        grad_act = act_a[...].astype(F32) + act_b[...].astype(F32)
        sigmoid_gate = jax.nn.sigmoid(pre_gate)
        activated = (pre_gate * sigmoid_gate * pre_up).astype(BF)
        by_gate = grad_act * pre_up * sigmoid_gate * (1.0 + pre_gate * (1.0 - sigmoid_gate))
        by_up = grad_act * pre_gate * sigmoid_gate
        gate_grad[...] = by_gate.astype(BF)
        up_grad[...] = by_up.astype(BF)
        weight_dot = jnp.sum(activated.astype(F32) * grad_act, axis=1, keepdims=True)
        mean_dot = jnp.sum(by_gate * pre_gate + by_up * pre_up, axis=1, keepdims=True)
        lane = lax.broadcasted_iota(jnp.int32, (done_ref.shape[0], 128), 1)
        sums = jnp.zeros(lane.shape, F32)
        for at, part in enumerate(in_pieces(weight_dot) + in_pieces(mean_dot)):
            sums = jnp.where((lane >= at * top_k) & (lane < (at + 1) * top_k), part, sums)
        out_ref[:, :, 2 * half_dim :] = sums.astype(BF).reshape(peers, per_peer, 128)
        out_ref[:, :, :half_dim] = done_ref[...].reshape(peers, per_peer, half_dim)

    columns = pl.ds(pl.multiple_of(half_dim + step * block, 128), block)
    part = contract_last(gate_grad[...], gate_ref[...]) + contract_last(up_grad[...], up_ref[...])
    out_ref[:, :, columns] = part.astype(BF).reshape(peers, per_peer, block)


def grad_parts(own_pre, other_pre, own_act, other_act, expert_out, gate_mat, up_mat, peers, top_k):
    slots, ff_dim = own_act.shape
    half_dim = gate_mat.shape[0]
    block = column_block(half_dim)
    shape = (peers, slots // peers, 2 * half_dim + 128)
    whole = lambda width: pl.BlockSpec((slots, width), lambda i: (0, 0))
    weights = pl.BlockSpec((block, ff_dim), lambda i: (i, 0))

    def body(*refs):
        part_kernel(top_k, *refs)

    return pl.pallas_call(
        body,
        grid=(half_dim // block,),
        in_specs=[whole(2 * ff_dim)] * 2 + [whole(ff_dim)] * 2 + [whole(half_dim)] + [weights] * 2,
        out_specs=pl.BlockSpec(shape, lambda i: (0, 0, 0)),
        out_shape=jax.ShapeDtypeStruct(shape, BF),
        scratch_shapes=[pltpu.VMEM((slots, ff_dim), BF)] * 2,
        compiler_params=room(40),
        cost_estimate=SMALL,
        name="grad_parts",
    )(own_pre, other_pre, own_act, other_act, expert_out, gate_mat, up_mat)


def finish_kernel(
    top_k,
    full_dim,
    out_rows,
    grad_rows,
    sum_rows,
    weights_ref,
    select_ref,
    slot_k_ref,
    inv_ref,
    tokens_ref,
    gain_ref,
    routed_ref,
    grad_ref,
    slot_ref,
    mean_ref,
):
    tok_dev = inv_ref.shape[0]
    slots = select_ref.shape[1]

    @pl.when(pl.program_id(0) == 0)
    def _():
        lane = lax.broadcasted_iota(jnp.int32, (slots, 128), 1)
        sums = sum_rows[...].reshape(slots, 128).astype(F32)
        sums = jnp.where((lane % top_k).astype(F32) == slot_k_ref[...], sums, 0.0).astype(BF)
        tail = jnp.dot(select_ref[...], sums, preferred_element_type=F32)
        slot_ref[...] = tail
        at = lax.broadcasted_iota(jnp.int32, tail.shape, 1)
        mean = jnp.where((at >= 3 * top_k) & (at < 6 * top_k), tail, 0.0)
        mean = jnp.sum(mean, axis=1, keepdims=True) / inv_ref[...] / full_dim
        mean_ref[...] = jnp.broadcast_to(mean, mean_ref.shape)

    outs = out_rows[...].reshape(slots, routed_ref.shape[1])
    halves = jnp.dot(weights_ref[...], outs, preferred_element_type=F32)
    routed_ref[...] = (halves[:tok_dev] + halves[tok_dev:]).astype(BF)
    grads = grad_rows[...].reshape(slots, routed_ref.shape[1])
    scaled = jnp.dot(select_ref[...], grads, preferred_element_type=F32) * gain_ref[...]
    inv = inv_ref[...]
    drop = tokens_ref[...].astype(F32) * (inv * inv * inv) * mean_ref[:, :1]
    grad_ref[...] = (inv * scaled - drop).astype(BF)


def finish(back, weights_t, select_t, slot_k, inv_rms, tokens, gain, top_k, full_dim):
    peers, per_peer, _ = back.shape
    tok_dev, half_dim = tokens.shape
    slots = peers * per_peer
    block = column_block(half_dim)
    steps = half_dim // block
    fixed = lambda shape: pl.BlockSpec(shape, lambda i: (0, 0))
    moving = lambda rows: pl.BlockSpec((rows, block), lambda i: (0, i))

    def body(*refs):
        finish_kernel(top_k, full_dim, *refs)

    return pl.pallas_call(
        body,
        grid=(steps,),
        in_specs=[
            pl.BlockSpec((peers, per_peer, block), lambda i: (0, 0, i)),
            pl.BlockSpec((peers, per_peer, block), lambda i: (0, 0, steps + i)),
            pl.BlockSpec((peers, per_peer, 128), lambda i: (0, 0, 2 * half_dim // 128)),
            fixed((2 * tok_dev, slots)),
            fixed((tok_dev, slots)),
            fixed((slots, 1)),
            fixed((tok_dev, 1)),
            moving(tok_dev),
            moving(1),
        ],
        out_specs=[moving(tok_dev), moving(tok_dev), fixed((tok_dev, 128))],
        out_shape=[
            jax.ShapeDtypeStruct((tok_dev, half_dim), BF),
            jax.ShapeDtypeStruct((tok_dev, half_dim), BF),
            jax.ShapeDtypeStruct((tok_dev, 128), F32),
        ],
        scratch_shapes=[pltpu.VMEM((tok_dev, 128), F32)],
        compiler_params=room(16),
        cost_estimate=SMALL,
        name="finish",
    )(back, back, back, weights_t, select_t, slot_k, inv_rms, tokens, gain.reshape(1, half_dim))


def rounded(value):
    return lax.reduce_precision(value, exponent_bits=8, mantissa_bits=7)


def blocks(rows, devices):
    return rows.reshape(devices, rows.shape[0] // devices, rows.shape[1])


def exchange(blocked, axes):
    return lax.all_to_all(blocked, axes, split_axis=0, concat_axis=0, tiled=True)


def local(tokens, gain, routes, route_weights, w_gate, w_up, w_down, grad_out):
    tok_dev, half_dim = tokens.shape
    top_k = routes.shape[1]
    section_size = lax.axis_size("section")
    full_dim = half_dim * section_size
    experts = lax.axis_size("tp") * lax.axis_size("zy") * CORES
    cap_src = max(2, tok_dev * top_k // experts + 1)
    slots = experts * cap_src
    gate_mat, up_mat, down_mat = (w_gate[0], w_up[0], w_down[0])
    ff_dim = gate_mat.shape[1]
    swap = [(i, (i + 1) % section_size) for i in range(section_size)]

    flip = [(0, 1), (1, 0)]
    mate_routes = lax.ppermute(routes, "core", flip)
    routes_t = routes.T
    weights_t = route_weights.T
    slot = lax.broadcasted_iota(jnp.int32, (slots, tok_dev), 0)
    expert_of, rank_of = slot // cap_src, slot % cap_src
    named = [routes_t[k : k + 1, :] == expert_of for k in range(top_k)]
    member = sum(n.astype(F32) for n in named)
    earlier = lax.broadcasted_iota(jnp.int32, (tok_dev, tok_dev), 0) < lax.broadcasted_iota(
        jnp.int32, (tok_dev, tok_dev), 1
    )
    rank = jnp.dot(member.astype(BF), earlier.astype(BF), preferred_element_type=F32)
    at_rank = rank == rank_of.astype(F32)
    picked = jnp.where(at_rank, member, 0.0)
    select = picked.astype(BF)
    weighted = sum(
        jnp.where(named[k] & at_rank, weights_t[k : k + 1, :], 0.0) for k in range(top_k)
    )

    core = lax.axis_index("core")
    chips = experts // CORES
    pair = CORES * tok_dev
    tokens_f = tokens.astype(F32)
    squares = jnp.sum(tokens_f * tokens_f, axis=1, keepdims=True)
    other_squares = lax.ppermute(squares, "section", swap)
    mate_tokens = lax.ppermute(tokens, "core", flip)
    mate_other = lax.ppermute(squares, ("section", "core"), [(i, 3 - i) for i in range(4)])
    mate_weights = lax.ppermute(route_weights, "core", flip)
    mate_grad = lax.ppermute(grad_out, "core", flip)
    mate_f = mate_tokens.astype(F32)
    mate_squares = jnp.sum(mate_f * mate_f, axis=1, keepdims=True)
    inv_rms = lax.rsqrt((squares + other_squares) / full_dim + EPS)
    mate_inv = lax.rsqrt((mate_squares + mate_other) / full_dim + EPS)

    pair_routes = jnp.concatenate([routes_t, mate_routes.T], axis=1)
    pair_weights = jnp.concatenate([weights_t, mate_weights.T], axis=1)
    row = lax.broadcasted_iota(jnp.int32, (slots, pair), 0)
    column = lax.broadcasted_iota(jnp.int32, (slots, pair), 1)
    wanted = row // (CORES * cap_src) * CORES + core
    here = row // cap_src % CORES == (column // tok_dev + core) % CORES
    pair_named = [(pair_routes[k : k + 1, :] == wanted) & here for k in range(top_k)]
    pair_member = sum(n.astype(F32) for n in pair_named)
    before = lax.broadcasted_iota(jnp.int32, (pair, pair), 0)
    after = lax.broadcasted_iota(jnp.int32, (pair, pair), 1)
    pair_earlier = (before // tok_dev == after // tok_dev) & (before < after)
    pair_rank = jnp.dot(
        pair_member.astype(BF), pair_earlier.astype(BF), preferred_element_type=F32
    )
    pair_at = pair_rank == (row % cap_src).astype(F32)
    pair_select = jnp.where(pair_at, pair_member, 0.0).astype(BF)
    pair_weighted = sum(
        jnp.where(n & pair_at, pair_weights[k : k + 1, :], 0.0)
        for k, n in enumerate(pair_named)
    )
    slot_weight = jnp.sum(pair_weighted, axis=1, keepdims=True)

    between = ("tp", "zy")
    messages = token_messages(pair_select, tokens, mate_tokens, inv_rms, mate_inv, gain, chips)
    arrived = exchange(messages, between).reshape(slots, half_dim)
    grad_pair = jnp.concatenate([grad_out, mate_grad], axis=0)
    grad_rows = (
        slot_weight * jnp.dot(pair_select, grad_pair, preferred_element_type=F32)
    ).astype(BF)
    grad_blocks = exchange(blocks(grad_rows, chips), between)

    own_pre = rounded(
        jnp.concatenate(
            [
                jnp.dot(arrived, gate_mat, preferred_element_type=F32),
                jnp.dot(arrived, up_mat, preferred_element_type=F32),
            ],
            axis=1,
        )
    )
    pre_send = own_pre.astype(BF)
    other_pre = lax.ppermute(pre_send, "section", swap)
    pre = own_pre + other_pre.astype(F32)
    pre_gate, pre_up = pre[:, :ff_dim], pre[:, ff_dim:]
    sigmoid_gate = jax.nn.sigmoid(pre_gate)
    activated = lax.optimization_barrier((pre_gate * sigmoid_gate * pre_up).astype(BF))
    expert_out = jnp.dot(activated, down_mat, preferred_element_type=F32).astype(BF)
    own_act = grad_act_part(grad_blocks, down_mat)
    other_act = lax.ppermute(own_act, "section", swap)
    parts = grad_parts(
        pre_send, other_pre, own_act, other_act, expert_out, gate_mat, up_mat, experts, top_k
    )
    back = exchange(parts, ("tp", "zy", "core"))

    weight_high = rounded(weighted)
    weight_low = weighted - weight_high
    slot_k = jnp.sum(
        sum(jnp.where(n & at_rank, float(k), 0.0) for k, n in enumerate(named)),
        axis=1,
        keepdims=True,
    )
    weights_both = jnp.concatenate([weight_high, weight_low], axis=1).astype(BF).T
    routed, grad_tokens, tail = finish(
        back, weights_both, select.T, slot_k, inv_rms, tokens, gain, top_k, full_dim
    )
    slot_dot = tail[:, :top_k] + tail[:, top_k : 2 * top_k] + tail[:, 2 * top_k : 3 * top_k]
    grad_weights = slot_dot / route_weights
    return (routed, grad_tokens, grad_weights)


def solution(mesh):
    sizes = mesh.shape
    shape = (sizes["section"], sizes["tp"], sizes["ep"] // CORES, CORES)
    fine = Mesh(mesh.devices.reshape(shape), ("section", "tp", "zy", "core"))
    rows = ("tp", "zy", "core")
    return jax.shard_map(
        local,
        mesh=fine,
        in_specs=(
            P(rows, "section"),
            P("section"),
            P(rows, None),
            P(rows, None),
            P(rows, "section", None),
            P(rows, "section", None),
            P(rows, None, "section"),
            P(rows, "section"),
        ),
        out_specs=(P(rows, "section"), P(rows, "section"), P(rows, None)),
        check_vma=False,
    )
```
